256 devices in a mesh: tile: 64 (over z, x, core), wp: 4 (over y).
Axes of the slice: x: 4, y: 4, z: 8, core: 2. Of those that a mesh axis runs over, the one named last changes fastest.
Arguments:
- visibilities: float32 [65536, 2, 128], P(('tile', 'wp')), may hold values from -6 to 6
- vis_weight: float32 [65536, 128], P(('tile', 'wp')), may hold values from 0.2 to 5
- cell_index: int32 [65536, 128], P(('tile', 'wp')), may hold values from 0 to 4095
- tap_offsets: int32 [65536, 128], P(('tile', 'wp')), may hold values from 0 to 255
- routes: int32 [65536, 1], P(('tile', 'wp')), may hold values from 0 to 255; in each aligned block of 256 rows (0 to 255, 256 to 511, ...) at most 2 rows name the same one
- patch_index: int32 [65536], P(('tile', 'wp')), may hold values from 0 to 255
- kernel: float32 [16, 8], replicated, may hold values from 0.1 to 1
Outputs:
- uv_grid: float32 [4, 64, 2, 1024, 1024], P('wp', 'tile')
The draws below stay inside these ranges and needn't reach their ends.
Inputs may be any that keep to these rules, and one draw needn't show every extreme that they name: `routes`: the 256 blocks of one device name no value more than 2 times, a bound that some block reaches.
All inputs are finite; a program needn't handle non-finite values.
Results may differ from the reference program's by a relative error of at most 0.0003.
Values sent between devices are 32-bit elements; how exact they have to be, the bound alone decides.
A program may use at most 192 MiB of HBM per device.

```python
import math
import jax
import jax.numpy as jnp
import numpy as np
from jax import lax

GRID = 8192
TCOLS = 8
SUB = 64
KW = 8
OVER = 16
ROWS = 128
BLK_DEV = 256
TILE = 1024
TILES = 64
NU = 8192
NW = 4
BLOCKS = 65536
CAP = 2
SIDE = 16


def touch_ends(values, key, least, top_value):
    spot = [jax.random.randint(jax.random.fold_in(key, axis), (), 0, length) for axis, length in enumerate(values.shape)]
    widest = values.shape.index(max(values.shape))
    beside = spot[:widest] + [(spot[widest] + 1) % values.shape[widest]] + spot[widest + 1:]
    return values.at[tuple(spot)].set(least).at[tuple(beside)].set(top_value)


def shard_levels(key, shape, shards, smallest, top_value):
    factor_of = 1.0
    for dim, shards_of in shards:
        steps = jax.random.uniform(jax.random.fold_in(jax.random.fold_in(key, 6), dim), (shards_of,), jnp.float32, smallest / len(shards), top_value / len(shards))
        factor_of = factor_of * jnp.repeat(jnp.exp(steps), shape[dim] // shards_of).reshape((-1,) + (1,) * (len(shape) - 1 - dim))
    return factor_of


def shared_out(stream_key, own, number, rows, number_of, top, reach, lean):
    sequence = jax.random.permutation(stream_key, number_of)
    crowded, ordinary = portions_of(number_of, rows * top, reach, lean, True), portions_of(number_of, rows * top, reach, lean, False)
    places = jnp.arange(number_of)

    def named(tallies, turn):
        used = int((tallies > 0).sum())
        fixed = max(1, used // 4)
        shifted = fixed + (places - fixed + turn * (used - fixed)) % max(1, number_of - fixed)
        return jnp.zeros((number_of,), jnp.int32).at[sequence[jnp.where(places < fixed, places, shifted)]].set(jnp.asarray(tallies, jnp.int32))

    tallies = jnp.where(number % 4 == 0, named(crowded, number // 4), named(ordinary, number - number // 4 - 1))
    mixed = jax.random.permutation(jax.random.fold_in(own, 3), number_of)
    giver, receiver = mixed[0:number_of // 2 * 2:2], mixed[1:number_of // 2 * 2:2]
    room = jnp.minimum(tallies[giver] - 1, reach - tallies[receiver]) // 2
    room = jnp.where((giver == sequence[0]) | (receiver == sequence[0]) | (tallies[receiver] == 0), 0, jnp.maximum(room, 0))
    shifted = jax.random.randint(jax.random.fold_in(own, 4), (number_of // 2,), 0, 1 << 20) % (room + 1)
    tallies = tallies.at[giver].add(-shifted).at[receiver].add(shifted)
    members = jnp.searchsorted(jnp.cumsum(tallies), jnp.arange(rows * top), side="right").astype(jnp.int32)
    table = members.reshape(top, rows).T
    table = table[jax.random.permutation(jax.random.fold_in(own, 1), rows)]
    turn = jax.random.randint(jax.random.fold_in(own, 2), (rows, 1), 0, top)
    return jnp.take_along_axis(table, (jnp.arange(top)[None, :] + turn) % top, axis=1)


def portions_of(number_of, total, most, slope, full):
    weights = [(1 << 20) // math.isqrt(standing ** slope) + 1 for standing in range(1, number_of + 1)]
    largest = most if full else min(most, max(-(-total // number_of), total * weights[0] // sum(weights)))
    least = 1 if total - largest >= number_of - 1 else 0
    counts, surplus = [largest] + [least] * (number_of - 1), total - largest - least * (number_of - 1)
    while surplus > 0:
        free = [i for i in range(1, number_of) if counts[i] < largest] or [i for i in range(1, number_of) if counts[i] < most]
        whole, left = sum([weights[i] for i in free]), surplus
        for i in free:
            extra = min(most - counts[i], max(1, left * weights[i] // whole), surplus)
            counts[i] = counts[i] + extra
            surplus = surplus - extra
    return np.array(counts)


def gaussian(rng, extent, scale, bound, split=(), held_as=jnp.bfloat16):
    entries = scale * jax.random.normal(rng, extent, jnp.float32)
    if split:
        entries = entries * shard_levels(rng, extent, split, -0.22, 0.18)
    return jnp.clip(entries, -bound, bound).astype(held_as)


def setup_inputs(seed: int = 0) -> dict:
    streams_of = jax.random.split(jax.random.key(seed), 8)
    visibilities = gaussian(streams_of[0], (BLOCKS, 2, ROWS), 1.0, 6.0, ((0, 256),), jnp.float32)
    vis_weight = jnp.clip(jnp.exp(math.log(5.0) - 3.218876 * jax.random.uniform(streams_of[1], (BLOCKS, ROWS), jnp.float32) ** shard_levels(streams_of[1], (BLOCKS, ROWS), ((0, 256),), -0.2, 0.2)), 0.2, 5.0)
    cell_index = touch_ends(jax.random.randint(streams_of[2], (BLOCKS, ROWS), 0, SUB * SUB), jax.random.fold_in(streams_of[2], 1), 0, (SUB * SUB) - 1).astype(jnp.int32)
    tap_offsets = touch_ends(jax.random.randint(streams_of[3], (BLOCKS, ROWS), 0, OVER * OVER), jax.random.fold_in(streams_of[3], 1), 0, (OVER * OVER) - 1).astype(jnp.int32)
    routes_keys = jax.random.split(jax.random.fold_in(streams_of[4], 1), BLOCKS // BLK_DEV)
    routes_turns = jax.random.permutation(jax.random.fold_in(streams_of[4], 3), BLOCKS // BLK_DEV)
    routes = jax.vmap(lambda own, number: shared_out(jax.random.fold_in(streams_of[4], 2), own, number, BLK_DEV, NW * TILES, 1, CAP, 2))(routes_keys, routes_turns).reshape((BLOCKS, 1))
    patch_index = touch_ends(jax.random.randint(streams_of[5], (BLOCKS,), 0, SIDE * SIDE), jax.random.fold_in(streams_of[5], 1), 0, (SIDE * SIDE) - 1).astype(jnp.int32)
    kernel = jnp.clip(jnp.exp(jax.random.uniform(streams_of[6], (OVER, KW), jnp.float32, math.log(0.1), math.log(1.0))), 0.1, 1.0)
    return dict(visibilities=visibilities, vis_weight=vis_weight, cell_index=cell_index, tap_offsets=tap_offsets, routes=routes, patch_index=patch_index, kernel=kernel)


def reference(visibilities, vis_weight, cell_index, tap_offsets, routes, patch_index, kernel):
    rows_u = NU + KW
    cols_v = GRID + KW
    target = routes[:, 0]
    w_plane = target % NW
    owner_tile = target // NW
    base_row = (owner_tile // TCOLS) * TILE + (patch_index // SIDE) * SUB
    base_col = (owner_tile % TCOLS) * TILE + (patch_index % SIDE) * SUB
    groups = BLOCKS // BLK_DEV
    tap_steps = jnp.arange(KW, dtype=jnp.int32)
    components = jnp.arange(2, dtype=jnp.int32)

    def regroup(values):
        return values.reshape((groups, BLK_DEV) + values.shape[1:])

    def add_group(flat_grid, group):
        group_vis, group_weight, group_cell, group_offset, group_row, group_col, group_plane = group
        kern_u = kernel[group_offset // OVER]
        kern_v = kernel[group_offset % OVER]
        scaled = group_vis * group_weight[:, None, :]
        contribution = scaled[:, :, :, None, None] * kern_u[:, None, :, :, None] * kern_v[:, None, :, None, :]
        pos_u = group_row[:, None] + group_cell // SUB
        pos_v = group_col[:, None] + group_cell % SUB
        flat_index = (group_plane[:, None, None, None, None] * 2 + components[None, :, None, None, None]) * rows_u
        flat_index = (flat_index + pos_u[:, None, :, None, None] + tap_steps[None, None, None, :, None]) * cols_v
        flat_index = flat_index + pos_v[:, None, :, None, None] + tap_steps[None, None, None, None, :]
        return flat_grid.at[flat_index.reshape(-1)].add(contribution.reshape(-1)), None

    flat_grid = jnp.zeros((NW * 2 * rows_u * cols_v,), jnp.float32)
    inputs = (regroup(visibilities), regroup(vis_weight), regroup(cell_index), regroup(tap_offsets),
              regroup(base_row), regroup(base_col), regroup(w_plane))
    flat_grid, _ = lax.scan(add_group, flat_grid, inputs)
    uv_grid = flat_grid.reshape(NW, 2, rows_u, cols_v)[:, :, :NU, :GRID]
    uv_grid = uv_grid.reshape(NW, 2, NU // TILE, TILE, TCOLS, TILE)
    uv_grid = jnp.transpose(uv_grid, (0, 2, 4, 1, 3, 5))
    return uv_grid.reshape(NW, TILES, 2, TILE, TILE)
```

```python
import functools

import jax
import jax.numpy as jnp
from jax import lax
from jax.experimental import pallas as pl
from jax.experimental.pallas import tpu as pltpu
from jax.sharding import PartitionSpec as P

TCOLS = 8
SUB = 64
KW = 8
OVER = 16
TILE = 1024
SIDE = TILE // SUB
PATCHES = SIDE * SIDE
EXT = SUB + KW
BLOCKS = 256
ZS, XS, YS, CORES = 8, 4, 4, 2
FAR = [(dz, dc) for dz in (4, 3, 5, 2, 6, 1, 7, 0) for dc in (0, 1)]
FAR = [step for step in FAR if step != (0, 0)] + [(0, 0)]
NEAR = [(dx, dy) for dx in (2, 1, 3, 0) for dy in (2, 1, 3, 0)]
GROUP = 16
HALVES = 2
MESH = pl.DeviceIdType.MESH
bf16, f32, i32 = jnp.bfloat16, jnp.float32, jnp.int32


def position():
    tile, y = lax.axis_index("tile"), lax.axis_index("wp")
    return tile // (XS * CORES), (tile // CORES) % XS, tile % CORES, y


def exchange_kernel(source_ref, patch_ref, vis_ref, weight_ref, cell_ref, tap_ref, got_ref,
                    outgoing, middle, far_out, far_in, near_out, near_in, local):
    z, x, core, y = position()

    def far_device(step, sign=1):
        dz, dc = step
        return ((((z + sign * dz + ZS) % ZS) * XS + x) * CORES + (core + dc) % CORES, y)

    def near_device(step, sign=1):
        dx, dy = step
        return ((z * XS + (x + sign * dx + XS) % XS) * CORES + core, (y + sign * dy + YS) % YS)

    barrier = pltpu.get_barrier_semaphore()
    for step in FAR[:-1]:
        pl.semaphore_signal(barrier, inc=1, device_id=far_device(step), device_id_type=MESH)
    for step in NEAR[:-1]:
        pl.semaphore_signal(barrier, inc=1, device_id=near_device(step), device_id_type=MESH)

    lane = lax.broadcasted_iota(i32, (1, 128), 1)

    def fill(far_index):
        dz, dc = FAR[far_index]
        to_z, to_core = (z + dz) % ZS, (core + dc) % CORES

        def one(near_index, carry):
            group = near_index // YS
            dx = jnp.where(group == 0, 2, jnp.where(group == 1, 1, jnp.where(group == 2, 3, 0)))
            group = near_index % YS
            dy = jnp.where(group == 0, 2, jnp.where(group == 1, 1, jnp.where(group == 2, 3, 0)))
            target = ((to_z * XS + (x + dx) % XS) * CORES + to_core) * YS + (y + dy) % YS
            spot = 2 * (near_index * GROUP + far_index) % 128
            patches = jnp.zeros((1, 128), i32)
            for slot in range(2):
                block = source_ref[slot, target]
                valid = jnp.where(block < BLOCKS, 1.0, 0.0).astype(f32)
                block = jnp.minimum(block, BLOCKS - 1)
                weight = weight_ref[pl.ds(block, 1), :] * valid
                outgoing[far_index, near_index, 3 * slot:3 * slot + 2, :] = vis_ref[block] * weight
                code = cell_ref[pl.ds(block, 1), :] * (OVER * OVER) + tap_ref[pl.ds(block, 1), :]
                outgoing[far_index, near_index, 3 * slot + 2:3 * slot + 3, :] = code.astype(f32)
                patches = jnp.where(lane == spot + slot, patch_ref[block], patches)
            outgoing[far_index, near_index, 6:7, :] = patches.astype(f32)
            outgoing[far_index, near_index, 7:8, :] = jnp.zeros((1, 128), f32)
            return carry

        lax.fori_loop(0, GROUP, one, 0, unroll=4)

    copies = []
    for index, step in enumerate(FAR):
        fill(index)
        if index == 0:
            pl.semaphore_wait(barrier, len(FAR) + len(NEAR) - 2)
        if index < GROUP - 1:
            copy = pltpu.make_async_remote_copy(
                src_ref=outgoing.at[index], dst_ref=middle.at[index],
                send_sem=far_out.at[index], recv_sem=far_in.at[index],
                device_id=far_device(step), device_id_type=MESH)
        else:
            copy = pltpu.make_async_copy(outgoing.at[index], middle.at[index], local.at[0])
        copy.start()
        copies.append(copy)

    part = GROUP // HALVES
    sends = []
    for half in range(HALVES):
        rows = pl.ds(half * part, part)
        for index in range(half * part, (half + 1) * part):
            if index < GROUP - 1:
                copies[index].wait_recv()
            else:
                copies[index].wait()
        for index, step in enumerate(NEAR):
            number = half * GROUP + index
            if index < GROUP - 1:
                copy = pltpu.make_async_remote_copy(
                    src_ref=middle.at[rows, index], dst_ref=got_ref.at[index, rows],
                    send_sem=near_out.at[number], recv_sem=near_in.at[number],
                    device_id=near_device(step), device_id_type=MESH)
            else:
                copy = pltpu.make_async_copy(
                    middle.at[rows, index], got_ref.at[index, rows], local.at[1 + half])
            copy.start()
            sends.append(copy)
    for copy in sends:
        copy.wait()
    for copy in copies[:-1]:
        copy.wait_send()


def exchange(source, patch_index, visibilities, vis_weight, cell_index, tap_offsets):
    vmem, smem = pl.BlockSpec(memory_space=pltpu.VMEM), pl.BlockSpec(memory_space=pltpu.SMEM)
    shape = (GROUP, GROUP, 8, 128)
    return pl.pallas_call(
        exchange_kernel,
        out_shape=jax.ShapeDtypeStruct(shape, f32),
        in_specs=[smem, smem] + [vmem] * 4,
        out_specs=vmem,
        scratch_shapes=[
            pltpu.VMEM(shape, f32), pltpu.VMEM(shape, f32),
            pltpu.SemaphoreType.DMA((GROUP,)), pltpu.SemaphoreType.DMA((GROUP,)),
            pltpu.SemaphoreType.DMA((HALVES * GROUP,)), pltpu.SemaphoreType.DMA((HALVES * GROUP,)),
            pltpu.SemaphoreType.DMA((1 + HALVES,)),
        ],
        compiler_params=pltpu.CompilerParams(
            collective_id=0, has_side_effects=True, vmem_limit_bytes=32 << 20),
    )(source, patch_index, visibilities, vis_weight, cell_index, tap_offsets)


UNROLL = 16
ROWS = 2 * EXT


def place(cell, row):
    step = (cell - row + 15) >> 4
    inside = (step * 16 + row - cell) < KW
    return jnp.where(inside, step, 99).astype(jnp.int16)


def halves(value):
    high = value.astype(bf16).astype(f32)
    rest = value - high
    return (jnp.concatenate([high, high], 0).astype(bf16), jnp.concatenate([rest, rest], 0).astype(bf16))


def contract(left, right):
    return lax.dot_general(left, right, (((1,), (1,)), ((), ())), preferred_element_type=f32)


def grid_kernel(got_ref, table_ref, tile_ref, right_ref, lower_ref, corner_ref,
                total, patch_rows, patch_smem, stage, patch_sem, stage_sem):
    for quarter in range(4):
        rows = jnp.sum(got_ref[pl.ds(quarter * 64, 64), 6, :], axis=0, keepdims=True)
        patch_rows[quarter:quarter + 1, :] = rows.astype(i32)
    numbers = pltpu.make_async_copy(patch_rows, patch_smem, patch_sem)
    numbers.start()

    def clear(k, carry):
        total[pl.ds(k * 4, 4)] = jnp.zeros((4, ROWS, 128), f32)
        return carry

    lax.fori_loop(0, (PATCHES + SIDE) // 4, clear, 0)
    numbers.wait()

    row8 = lax.broadcasted_iota(i32, (8, 128), 0)
    row16 = lax.broadcasted_iota(i32, (16, 128), 0)
    table = table_ref[...]
    zero = jnp.zeros((16, 128), bf16)

    def spread(masks, value):
        return jnp.concatenate([jnp.where(mask, value, zero) for mask in masks], 0)

    def one(pair, slot):
        real = got_ref[pair, pl.ds(3 * slot, 1), :]
        imag = got_ref[pair, pl.ds(3 * slot + 1, 1), :]
        code = jnp.broadcast_to(got_ref[pair, pl.ds(3 * slot + 2, 1), :], (8, 128)).astype(i32)
        cell_u = code >> 14
        cell_v = (code >> 8) & (SUB - 1)
        ku = jnp.take_along_axis(table, ((code >> 1) & 0x78) + ((row8 - cell_u) & 7), axis=1)
        kv = jnp.take_along_axis(table, ((code << 3) & 0x78) + ((row8 - cell_v) & 7), axis=1)
        step_u = place(jnp.concatenate([cell_u, cell_u], 0), row16)
        step_v = place(jnp.concatenate([cell_v, cell_v], 0), row16)
        masks_u = [step_u == jnp.int16(t) for t in range(5)]
        masks_v = [step_v == jnp.int16(t) for t in range(5)]
        v_high, v_rest = halves(kv)
        r_high, r_rest = halves(ku * real)
        i_high, i_rest = halves(ku * imag)
        v_high, v_rest = spread(masks_v, v_high), spread(masks_v, v_rest)
        u_high = jnp.concatenate([spread(masks_u, r_high), spread(masks_u, i_high)], 0)
        u_rest = jnp.concatenate([spread(masks_u, r_rest), spread(masks_u, i_rest)], 0)
        out = contract(jnp.concatenate([u_high, u_rest], 1), jnp.concatenate([v_high, v_high], 1))
        out = out + contract(u_high, v_rest)
        number = 2 * pair + slot
        patch = patch_smem[number // 128, number % 128] + SIDE
        total[patch, 0:EXT, 0:80] = total[patch, 0:EXT, 0:80] + out[0:EXT]
        total[patch, EXT:ROWS, 0:80] = total[patch, EXT:ROWS, 0:80] + out[80:80 + EXT]

    def several(k, carry):
        for q in range(UNROLL):
            for slot in range(2):
                one(k * UNROLL + q, slot)
        return carry

    lax.fori_loop(0, BLOCKS // UNROLL, several, 0)

    lane = lax.broadcasted_iota(i32, (8, 128), 1)
    right_ref[...] = jnp.zeros_like(right_ref)

    def joined(load, put):
        before = jnp.zeros((8, 128), f32)
        for pair in range(SIDE // 2):
            moved = pltpu.roll(load(2 * pair + 1), SUB, 1)
            put(pair, load(2 * pair) + jnp.where(lane >= SUB, moved, before))
            before = moved
        return jnp.where(lane < KW, before, 0.0)

    def stripe(patch_row, slot):
        for part in range(2):
            for step in range(SUB // 8):
                start = part * EXT + step * 8

                def load(column):
                    value = total[(patch_row + 1) * SIDE + column, start:start + 8, :]
                    if step == 0:
                        last = part * EXT + SUB
                        value = value + total[patch_row * SIDE + column, last:last + 8, :]
                    return value

                def put(pair, value):
                    stage[slot, part, step * 8:step * 8 + 8, pair * 128:pair * 128 + 128] = value

                past = joined(load, put)
                rows = slice(step * 8, step * 8 + 8)
                right_ref[part, rows, :] = right_ref[part, rows, :] + pltpu.roll(past, patch_row * KW, 1)

    def write(patch_row, slot):
        return pltpu.make_async_copy(
            stage.at[slot], tile_ref.at[:, pl.ds(patch_row * SUB, SUB), :], stage_sem.at[slot])

    def two(k, carry):
        for slot in range(2):
            @pl.when(k > 0)
            def _():
                write(2 * k - 2 + slot, slot).wait()
            stripe(2 * k + slot, slot)
            write(2 * k + slot, slot).start()
        return carry

    lax.fori_loop(0, SIDE // 2, two, 0)

    for part in range(2):
        last = part * EXT + SUB

        def load(column):
            return total[SIDE * SIDE + column, last:last + 8, :]

        def put(pair, value):
            lower_ref[part, :, pair * 128:pair * 128 + 128] = value

        corner_ref[part] = joined(load, put)
    for slot in range(2):
        write(SIDE - 2 + slot, slot).wait()


def make_tile(got, table):
    vmem = pl.BlockSpec(memory_space=pltpu.VMEM)
    return pl.pallas_call(
        grid_kernel,
        out_shape=(
            jax.ShapeDtypeStruct((2, TILE, TILE), f32), jax.ShapeDtypeStruct((2, SUB, 128), f32),
            jax.ShapeDtypeStruct((2, KW, TILE), f32), jax.ShapeDtypeStruct((2, KW, 128), f32)),
        in_specs=[vmem, vmem],
        out_specs=(pl.BlockSpec(memory_space=pl.ANY), vmem, vmem, vmem),
        scratch_shapes=[
            pltpu.VMEM((PATCHES + SIDE, ROWS, 128), f32),
            pltpu.VMEM((4, 128), i32), pltpu.SMEM((4, 128), i32),
            pltpu.VMEM((2, 2, SUB, TILE), f32),
            pltpu.SemaphoreType.DMA, pltpu.SemaphoreType.DMA((2,)),
        ],
        compiler_params=pltpu.CompilerParams(vmem_limit_bytes=48 << 20),
    )(got, table)


def margins_kernel(right_ref, lower_ref, corner_ref, left_in, upper_in, corner_in, out_sem, in_sem):
    tile, y = lax.axis_index("tile"), lax.axis_index("wp")
    tiles = ZS * XS * CORES
    barrier = pltpu.get_barrier_semaphore()
    steps = (1, TCOLS, TCOLS + 1)
    for step in steps:
        for to in ((tile + step) % tiles, (tile + tiles - step) % tiles):
            pl.semaphore_signal(barrier, inc=1, device_id=(to, y), device_id_type=MESH)
    pl.semaphore_wait(barrier, 2 * len(steps))
    copies = []
    for index, (source, target) in enumerate(
            ((right_ref, left_in), (lower_ref, upper_in), (corner_ref, corner_in))):
        copy = pltpu.make_async_remote_copy(
            src_ref=source, dst_ref=target, send_sem=out_sem.at[index], recv_sem=in_sem.at[index],
            device_id=((tile + steps[index]) % tiles, y), device_id_type=MESH)
        copy.start()
        copies.append(copy)
    for copy in copies:
        copy.wait()


def margins(right, lower, corner):
    vmem = pl.BlockSpec(memory_space=pltpu.VMEM)
    return pl.pallas_call(
        margins_kernel,
        out_shape=tuple(jax.ShapeDtypeStruct(a.shape, a.dtype) for a in (right, lower, corner)),
        in_specs=[vmem] * 3,
        out_specs=(vmem,) * 3,
        scratch_shapes=[pltpu.SemaphoreType.DMA((3,)), pltpu.SemaphoreType.DMA((3,))],
        compiler_params=pltpu.CompilerParams(collective_id=1, has_side_effects=True),
    )(right, lower, corner)


def finish_kernel(tile_in, left_in, upper_in, corner_in, tile_ref, side, top, sems):
    del tile_in
    tile = lax.axis_index("tile")
    has_left = jnp.where(tile % TCOLS > 0, 1.0, 0.0).astype(f32)
    has_upper = jnp.where(tile // TCOLS > 0, 1.0, 0.0).astype(f32)
    sides = tile_ref.at[:, :, pl.ds(0, 128)]
    tops = tile_ref.at[:, pl.ds(0, KW), pl.ds(128, TILE - 128)]
    read_side = pltpu.make_async_copy(sides, side, sems.at[0])
    read_top = pltpu.make_async_copy(tops, top, sems.at[1])
    read_side.start()
    read_top.start()
    lane = lax.broadcasted_iota(i32, (SUB, 128), 1)
    read_top.wait()
    top[...] = top[...] + upper_in[:, :, 128:] * has_upper
    write_top = pltpu.make_async_copy(top, tops, sems.at[1])
    write_top.start()
    read_side.wait()
    for part in range(2):
        packed = left_in[part] * has_left
        for patch_row in range(SIDE):
            rows = slice(patch_row * SUB, patch_row * SUB + SUB)
            moved = packed if patch_row == 0 else pltpu.roll(packed, 128 - KW * patch_row, 1)
            side[part, rows, :] = side[part, rows, :] + jnp.where(lane < KW, moved, 0.0)
        side[part, 0:KW, :] = (side[part, 0:KW, :] + upper_in[part, :, 0:128] * has_upper
                               + corner_in[part] * (has_left * has_upper))
    write_side = pltpu.make_async_copy(side, sides, sems.at[0])
    write_side.start()
    write_top.wait()
    write_side.wait()


def finish(tile, left, upper, corner):
    vmem, hbm = pl.BlockSpec(memory_space=pltpu.VMEM), pl.BlockSpec(memory_space=pl.ANY)
    return pl.pallas_call(
        finish_kernel,
        out_shape=jax.ShapeDtypeStruct(tile.shape, tile.dtype),
        in_specs=[hbm, vmem, vmem, vmem],
        out_specs=hbm,
        scratch_shapes=[
            pltpu.VMEM((2, TILE, 128), f32), pltpu.VMEM((2, KW, TILE - 128), f32),
            pltpu.SemaphoreType.DMA((2,))],
        input_output_aliases={0: 0},
        compiler_params=pltpu.CompilerParams(vmem_limit_bytes=16 << 20),
    )(tile, left, upper, corner)


def shards(visibilities, vis_weight, cell_index, tap_offsets, routes, patch_index, kernel):
    blocks = visibilities.shape[0]
    block_ids = lax.broadcasted_iota(i32, (blocks, blocks), 0)
    named = routes == lax.broadcasted_iota(i32, (blocks, blocks), 1)
    first = jnp.min(jnp.where(named, block_ids, blocks), axis=0)
    last = jnp.max(jnp.where(named, block_ids, -1), axis=0)
    source = jnp.stack([first, jnp.where(last > first, last, blocks)])
    got = exchange(source, patch_index, visibilities, vis_weight, cell_index, tap_offsets)
    table = jnp.broadcast_to(kernel.reshape(1, OVER * KW), (8, OVER * KW))
    tile, right, lower, corner = make_tile(got.reshape(BLOCKS, 8, 128), table)
    tile = finish(tile, *margins(right, lower, corner))
    return tile.reshape(1, 1, 2, TILE, TILE)


def solution(mesh):
    in_specs = (
        P(("tile", "wp"), None, None),
        P(("tile", "wp"), None),
        P(("tile", "wp"), None),
        P(("tile", "wp"), None),
        P(("tile", "wp"), None),
        P(("tile", "wp")),
        P(),
    )
    out_specs = P("wp", "tile", None, None, None)
    return jax.shard_map(shards, mesh=mesh, in_specs=in_specs, out_specs=out_specs, check_vma=False)
```

```python
import functools

import jax
import jax.numpy as jnp
from jax import lax
from jax.experimental import pallas as pl
from jax.experimental.pallas import tpu as pltpu
from jax.sharding import PartitionSpec as P

TCOLS = 8
SUB = 64
KW = 8
OVER = 16
TILE = 1024
SIDE = TILE // SUB
PATCHES = SIDE * SIDE
EXT = SUB + KW
BLOCKS = 256
ZS, XS, YS, CORES = 8, 4, 4, 2
GROUP = 16
LINES = 3 * GROUP + 2
EARLY = 8
MESH = pl.DeviceIdType.MESH
bf16, f32, i32 = jnp.bfloat16, jnp.float32, jnp.int32


def position():
    tile, y = lax.axis_index("tile"), lax.axis_index("wp")
    return tile // (XS * CORES), (tile // CORES) % XS, tile % CORES, y


def offset(order, size):
    if isinstance(order, int):
        return size // 2 + (order // 2 if order % 2 == 0 else -((order + 1) // 2))
    return size // 2 + jnp.where(order % 2 == 0, order // 2, -((order + 1) // 2))


def far_step(step):
    return offset(step // 2, ZS), (step + 1) % 2


def near_step(step):
    return offset(step // 4, XS), offset(step % 4, YS)


def exchange_kernel(source_ref, patch_ref, vis_any, weight_any, cell_any, tap_any,
                    got_far, got_near, patches_ref,
                    vis_ref, weight_ref, cell_ref, tap_ref,
                    far_data, near_data, far_middle, near_middle, far_lines, near_lines,
                    far_marks, near_marks, load_sem, local,
                    far_out1, far_in1, near_out1, near_in1, far_out2, far_in2, near_out2, near_in2,
                    far_out3, far_in3, near_out3, near_in3):
    z, x, core, y = position()
    own = GROUP - 1

    loads = []
    for index, (source, target) in enumerate((
            (vis_any, vis_ref), (weight_any, weight_ref), (cell_any, cell_ref), (tap_any, tap_ref))):
        load = pltpu.make_async_copy(source, target.at[pl.ds(0, BLOCKS)], load_sem.at[index])
        load.start()
        loads.append(load)
        target[BLOCKS:] = jnp.zeros_like(target[BLOCKS:])

    def far_device(step):
        dz, dc = far_step(step)
        return ((((z + dz) % ZS) * XS + x) * CORES + (core + dc) % CORES, y)

    def near_device(step):
        dx, dy = near_step(step)
        return ((z * XS + (x + dx) % XS) * CORES + core, (y + dy) % YS)

    barrier = pltpu.get_barrier_semaphore()
    for step in range(own):
        pl.semaphore_signal(barrier, inc=1, device_id=far_device(step), device_id_type=MESH)
        pl.semaphore_signal(barrier, inc=1, device_id=near_device(step), device_id_type=MESH)
    for load in loads:
        load.wait()

    lane = lax.broadcasted_iota(i32, (1, 128), 1)

    def fill(data, slot, first):
        def line(number, carry):
            marks = jnp.zeros((1, 128), i32)
            for k in range(8):
                second = number * 8 + k
                block = source_ref[slot, first * GROUP + second if slot == 0 else second * GROUP + first]
                weight = weight_ref[pl.ds(block, 1), :]
                data[first, 3 * second] = vis_ref[block, 0:1, :] * weight
                data[first, 3 * second + 1] = vis_ref[block, 1:2, :] * weight
                code = cell_ref[pl.ds(block, 1), :] * (OVER * OVER) + tap_ref[pl.ds(block, 1), :]
                data[first, 3 * second + 2] = code.astype(f32)
                patch = patch_ref[jnp.minimum(block, BLOCKS - 1)]
                marks = jnp.where(lane == first + GROUP * k, patch, marks)
            data[first, 3 * GROUP + number] = marks.astype(f32)
            return carry

        lax.fori_loop(0, 2, line, 0)

    def send(source, target, out_sem, in_sem, index, device):
        copy = pltpu.make_async_remote_copy(
            src_ref=source, dst_ref=target, send_sem=out_sem.at[index], recv_sem=in_sem.at[index],
            device_id=device, device_id_type=MESH)
        copy.start()
        return copy

    def keep(source, target, index):
        copy = pltpu.make_async_copy(source, target, local.at[index])
        copy.start()
        return copy

    far_first, near_first = [], []
    for step in range(GROUP):
        fill(far_data, 0, step)
        if step == 0:
            pl.semaphore_wait(barrier, 2 * own)
        if step < own:
            far_first.append(send(far_data.at[step], far_middle.at[step], far_out1, far_in1, step, far_device(step)))
        else:
            far_first.append(keep(far_data.at[step], far_middle.at[step], 0))
        fill(near_data, 1, step)
        if step < own:
            near_first.append(send(near_data.at[step], near_middle.at[step], near_out1, near_in1, step, near_device(step)))
        else:
            near_first.append(keep(near_data.at[step], near_middle.at[step], 1))

    def arrive(copies, middle, lines):
        for copy in copies[:own]:
            copy.wait_recv()
        copies[own].wait()
        for line in range(2):
            total = middle[0, 3 * GROUP + line]
            for step in range(1, GROUP):
                total = total + middle[step, 3 * GROUP + line]
            lines[line] = total

    def far_second(step):
        part = near_middle.at[:, pl.ds(3 * step, 3)]
        line = near_lines.at[step // 8]
        if step == own:
            return [keep(part, got_near.at[step], 2), keep(line, near_marks.at[step], 3)]
        return [send(part, got_near.at[step], far_out2, far_in2, step, far_device(step)),
                send(line, near_marks.at[step], far_out3, far_in3, step, far_device(step))]

    def near_second(step):
        part = far_middle.at[:, pl.ds(3 * step, 3)]
        line = far_lines.at[step // 8]
        if step == own:
            return [keep(part, got_far.at[step], 4), keep(line, far_marks.at[step], 5)]
        return [send(part, got_far.at[step], near_out2, near_in2, step, near_device(step)),
                send(line, far_marks.at[step], near_out3, near_in3, step, near_device(step))]

    second = []
    arrive(near_first, near_middle, near_lines)
    for step in range(EARLY):
        second += far_second(step)
    arrive(far_first, far_middle, far_lines)
    for step in range(GROUP):
        second += near_second(step)
        if step + EARLY < GROUP:
            second += far_second(step + EARLY)
    for copy in second:
        copy.wait()
    for copy in far_first[:own] + near_first[:own]:
        copy.wait_send()
    for row, marks in ((0, far_marks), (2, near_marks)):
        for line in range(2):
            total = jnp.zeros((1, 128), f32)
            for k in range(8):
                total = jnp.where(lane // GROUP == k, marks[line * 8 + k], total)
            patches_ref[row + line:row + line + 1, :] = total.astype(i32)


def exchange(source, patch_index, visibilities, vis_weight, cell_index, tap_offsets):
    smem, hbm = pl.BlockSpec(memory_space=pltpu.SMEM), pl.BlockSpec(memory_space=pl.ANY)
    got = jax.ShapeDtypeStruct((GROUP, GROUP, 3, 1, 128), f32)
    message = pltpu.VMEM((GROUP, LINES, 1, 128), f32)
    return pl.pallas_call(
        exchange_kernel,
        out_shape=(got, got, jax.ShapeDtypeStruct((4, 128), i32)),
        in_specs=[smem, smem] + [hbm] * 4,
        out_specs=(hbm, hbm, pl.BlockSpec(memory_space=pltpu.VMEM)),
        scratch_shapes=[
            pltpu.VMEM((BLOCKS + 8, 2, 128), f32), pltpu.VMEM((BLOCKS + 8, 128), f32),
            pltpu.VMEM((BLOCKS + 8, 128), i32), pltpu.VMEM((BLOCKS + 8, 128), i32),
            message, message, message, message,
            pltpu.VMEM((2, 1, 128), f32), pltpu.VMEM((2, 1, 128), f32),
            pltpu.VMEM((GROUP, 1, 128), f32), pltpu.VMEM((GROUP, 1, 128), f32),
            pltpu.SemaphoreType.DMA((4,)), pltpu.SemaphoreType.DMA((6,)),
        ] + [pltpu.SemaphoreType.DMA((GROUP,))] * 12,
        compiler_params=pltpu.CompilerParams(
            collective_id=0, has_side_effects=True, vmem_limit_bytes=60 << 20),
    )(source, patch_index, visibilities, vis_weight, cell_index, tap_offsets)


UNROLL = 32
ROWS = 2 * EXT
CHUNKS = 4


def halves(value):
    high = value.astype(bf16).astype(f32)
    rest = value - high
    return (jnp.concatenate([high, high], 0).astype(bf16), jnp.concatenate([rest, rest], 0).astype(bf16))


def contract(left, right):
    return lax.dot_general(left, right, (((1,), (1,)), ((), ())), preferred_element_type=f32)


def grid_kernel(patch_ref, far_any, near_any, table_ref, tile_ref, right_ref, lower_ref, corner_ref,
                total, got, stage, load_sem, stage_sem):
    loads = []
    for slot, source in enumerate((far_any, near_any)):
        load = pltpu.make_async_copy(source, got.at[slot], load_sem.at[slot])
        load.start()
        loads.append(load)

    def clear(k, carry):
        total[pl.ds(k * 4, 4)] = jnp.zeros((4, ROWS, 128), f32)
        return carry

    lax.fori_loop(0, (PATCHES + SIDE) // 4, clear, 0)
    for load in loads:
        load.wait()

    row8 = lax.broadcasted_iota(i32, (8, 128), 0)
    table = table_ref[...]
    zero = jnp.zeros((16, 128), bf16)

    def steps(cell):
        step = (cell + 7 - row8) >> 3
        return jnp.concatenate([step, step - 1], 0).astype(jnp.int16)

    def one(slot, index):
        real = got[slot, index, 0]
        imag = got[slot, index, 1]
        code = jnp.broadcast_to(got[slot, index, 2], (8, 128)).astype(i32)
        cell_u = code >> 14
        cell_v = (code >> 8) & (SUB - 1)
        ku = jnp.take_along_axis(table, ((code >> 1) & 0x78) + ((row8 - cell_u) & 7), axis=1)
        kv = jnp.take_along_axis(table, ((code << 3) & 0x78) + ((row8 - cell_v) & 7), axis=1)
        step_u, step_v = steps(cell_u), steps(cell_v)
        masks_u = [step_u == jnp.int16(2 * t) for t in range(5)]
        masks_v = [step_v == jnp.int16(2 * t) for t in range(5)]

        def rows_u(first, second):
            return jnp.concatenate(
                [jnp.where(mask, value, zero) for value in (first, second) for mask in masks_u], 0)

        def rows_v(value):
            return jnp.concatenate([jnp.where(mask, value, zero) for mask in masks_v], 0)

        v_high, v_rest = halves(kv)
        r_high, r_rest = halves(ku * real)
        i_high, i_rest = halves(ku * imag)
        v_high, v_rest = rows_v(v_high), rows_v(v_rest)
        u_high, u_rest = rows_u(r_high, i_high), rows_u(r_rest, i_rest)
        out = contract(jnp.concatenate([u_high, u_rest, u_high], 1),
                       jnp.concatenate([v_high, v_high, v_rest], 1))
        patch = patch_ref[2 * slot + index // 128, index % 128] + SIDE
        total[patch, 0:EXT, 0:80] = total[patch, 0:EXT, 0:80] + out[0:EXT]
        total[patch, EXT:ROWS, 0:80] = total[patch, EXT:ROWS, 0:80] + out[80:80 + EXT]

    def several(k, carry):
        for q in range(UNROLL):
            for slot in range(2):
                one(slot, k * UNROLL + q)
        return carry

    lax.fori_loop(0, BLOCKS // UNROLL, several, 0)

    lane = lax.broadcasted_iota(i32, (8, 128), 1)
    right_ref[...] = jnp.zeros_like(right_ref)

    def joined(load, put):
        before = jnp.zeros((8, 128), f32)
        for pair in range(SIDE // 2):
            moved = pltpu.roll(load(2 * pair + 1), SUB, 1)
            put(pair, load(2 * pair) + jnp.where(lane >= SUB, moved, before))
            before = moved
        return jnp.where(lane < KW, before, 0.0)

    def stripe(patch_row):
        for part in range(2):
            for step in range(SUB // 8):
                start = part * EXT + step * 8

                def load(column):
                    value = total[(patch_row + 1) * SIDE + column, start:start + 8, :]
                    if step == 0:
                        last = part * EXT + SUB
                        value = value + total[patch_row * SIDE + column, last:last + 8, :]
                    return value

                def put(pair, value):
                    place = pl.multiple_of(patch_row * SUB + step * 8, 8)
                    stage[part, pl.ds(place, 8), pair * 128:pair * 128 + 128] = value

                past = joined(load, put)
                rows = slice(step * 8, step * 8 + 8)
                right_ref[part, rows, :] = right_ref[part, rows, :] + pltpu.roll(past, patch_row * KW, 1)

    def each(patch_row, carry):
        stripe(patch_row)
        for part in range(2):
            for chunk in range(CHUNKS):
                rows = pl.ds(patch_row * SUB + chunk * (SUB // CHUNKS), SUB // CHUNKS)
                pltpu.make_async_copy(stage.at[part, rows], tile_ref.at[part, rows], stage_sem).start()
        return carry

    lax.fori_loop(0, SIDE, each, 0)

    for part in range(2):
        last = part * EXT + SUB

        def load(column):
            return total[SIDE * SIDE + column, last:last + 8, :]

        def put(pair, value):
            lower_ref[part, :, pair * 128:pair * 128 + 128] = value

        corner_ref[part] = joined(load, put)
    pltpu.make_async_copy(stage, tile_ref, stage_sem).wait()


def make_tile(patches, far, near, table):
    vmem, hbm = pl.BlockSpec(memory_space=pltpu.VMEM), pl.BlockSpec(memory_space=pl.ANY)
    return pl.pallas_call(
        grid_kernel,
        out_shape=(
            jax.ShapeDtypeStruct((2, TILE, TILE), f32), jax.ShapeDtypeStruct((2, SUB, 128), f32),
            jax.ShapeDtypeStruct((2, KW, TILE), f32), jax.ShapeDtypeStruct((2, KW, 128), f32)),
        in_specs=[pl.BlockSpec(memory_space=pltpu.SMEM), hbm, hbm, vmem],
        out_specs=(hbm, vmem, vmem, vmem),
        scratch_shapes=[
            pltpu.VMEM((PATCHES + SIDE, ROWS, 128), f32),
            pltpu.VMEM((2, BLOCKS, 3, 1, 128), f32),
            pltpu.VMEM((2, TILE, TILE), f32),
            pltpu.SemaphoreType.DMA((2,)), pltpu.SemaphoreType.DMA,
        ],
        compiler_params=pltpu.CompilerParams(vmem_limit_bytes=60 << 20),
    )(patches, far, near, table)


def margins_kernel(right_ref, lower_ref, corner_ref, left_in, upper_in, corner_in, out_sem, in_sem):
    tile, y = lax.axis_index("tile"), lax.axis_index("wp")
    tiles = ZS * XS * CORES
    barrier = pltpu.get_barrier_semaphore()
    steps = (1, TCOLS, TCOLS + 1)
    for step in steps:
        for to in ((tile + step) % tiles, (tile + tiles - step) % tiles):
            pl.semaphore_signal(barrier, inc=1, device_id=(to, y), device_id_type=MESH)
    pl.semaphore_wait(barrier, 2 * len(steps))
    copies = []
    for index, (source, target) in enumerate(
            ((right_ref, left_in), (lower_ref, upper_in), (corner_ref, corner_in))):
        copy = pltpu.make_async_remote_copy(
            src_ref=source, dst_ref=target, send_sem=out_sem.at[index], recv_sem=in_sem.at[index],
            device_id=((tile + steps[index]) % tiles, y), device_id_type=MESH)
        copy.start()
        copies.append(copy)
    for copy in copies:
        copy.wait()


def margins(right, lower, corner):
    hbm = pl.BlockSpec(memory_space=pl.ANY)
    return pl.pallas_call(
        margins_kernel,
        out_shape=tuple(jax.ShapeDtypeStruct(a.shape, a.dtype) for a in (right, lower, corner)),
        in_specs=[hbm] * 3,
        out_specs=(hbm,) * 3,
        scratch_shapes=[pltpu.SemaphoreType.DMA((3,)), pltpu.SemaphoreType.DMA((3,))],
        compiler_params=pltpu.CompilerParams(collective_id=1, has_side_effects=True, vmem_limit_bytes=60 << 20),
    )(right, lower, corner)


def finish_kernel(tile_in, left_any, upper_any, corner_any, tile_ref,
                  side, top, left_in, upper_in, corner_in, sems):
    del tile_in
    tile = lax.axis_index("tile")
    has_left = jnp.where(tile % TCOLS > 0, 1.0, 0.0).astype(f32)
    has_upper = jnp.where(tile // TCOLS > 0, 1.0, 0.0).astype(f32)
    sides = tile_ref.at[:, :, pl.ds(0, 128)]
    tops = tile_ref.at[:, pl.ds(0, KW), pl.ds(128, TILE - 128)]
    read_side = pltpu.make_async_copy(sides, side, sems.at[0])
    read_top = pltpu.make_async_copy(tops, top, sems.at[1])
    read_side.start()
    read_top.start()
    loads = []
    for index, (source, target) in enumerate(
            ((upper_any, upper_in), (left_any, left_in), (corner_any, corner_in))):
        load = pltpu.make_async_copy(source, target, sems.at[2 + index])
        load.start()
        loads.append(load)
    lane = lax.broadcasted_iota(i32, (SUB, 128), 1)
    read_top.wait()
    loads[0].wait()
    top[...] = top[...] + upper_in[:, :, 128:] * has_upper
    write_top = pltpu.make_async_copy(top, tops, sems.at[1])
    write_top.start()
    read_side.wait()
    loads[1].wait()
    loads[2].wait()
    for part in range(2):
        packed = left_in[part] * has_left
        for patch_row in range(SIDE):
            rows = slice(patch_row * SUB, patch_row * SUB + SUB)
            moved = packed if patch_row == 0 else pltpu.roll(packed, 128 - KW * patch_row, 1)
            side[part, rows, :] = side[part, rows, :] + jnp.where(lane < KW, moved, 0.0)
        side[part, 0:KW, :] = (side[part, 0:KW, :] + upper_in[part, :, 0:128] * has_upper
                               + corner_in[part] * (has_left * has_upper))
    write_side = pltpu.make_async_copy(side, sides, sems.at[0])
    write_side.start()
    write_top.wait()
    write_side.wait()


def finish(tile, left, upper, corner):
    hbm = pl.BlockSpec(memory_space=pl.ANY)
    return pl.pallas_call(
        finish_kernel,
        out_shape=jax.ShapeDtypeStruct(tile.shape, tile.dtype),
        in_specs=[hbm] * 4,
        out_specs=hbm,
        scratch_shapes=[
            pltpu.VMEM((2, TILE, 128), f32), pltpu.VMEM((2, KW, TILE - 128), f32),
            pltpu.VMEM(left.shape, f32), pltpu.VMEM(upper.shape, f32), pltpu.VMEM(corner.shape, f32),
            pltpu.SemaphoreType.DMA((5,))],
        input_output_aliases={0: 0},
        compiler_params=pltpu.CompilerParams(vmem_limit_bytes=60 << 20),
    )(tile, left, upper, corner)


def shards(visibilities, vis_weight, cell_index, tap_offsets, routes, patch_index, kernel):
    blocks = visibilities.shape[0]
    block_ids = lax.broadcasted_iota(i32, (blocks, blocks), 0)
    step = lax.broadcasted_iota(i32, (blocks, blocks), 1)
    z, x, core, y = position()
    (dz, dc), (dx, dy) = far_step(step // GROUP), near_step(step % GROUP)
    target = ((((z + dz) % ZS) * XS + (x + dx) % XS) * CORES + (core + dc) % CORES) * YS + (y + dy) % YS
    named = routes == target
    first = jnp.min(jnp.where(named, block_ids, blocks), axis=0)
    last = jnp.max(jnp.where(named, block_ids, -1), axis=0)
    source = jnp.stack([first, jnp.where(last > first, last, blocks)])
    far, near, patches = exchange(source, patch_index, visibilities, vis_weight, cell_index, tap_offsets)
    table = jnp.broadcast_to(kernel.reshape(1, OVER * KW), (8, OVER * KW))
    tile, right, lower, corner = make_tile(
        patches, far.reshape(BLOCKS, 3, 1, 128), near.reshape(BLOCKS, 3, 1, 128), table)
    tile = finish(tile, *margins(right, lower, corner))
    return tile.reshape(1, 1, 2, TILE, TILE)


def solution(mesh):
    in_specs = (
        P(("tile", "wp"), None, None),
        P(("tile", "wp"), None),
        P(("tile", "wp"), None),
        P(("tile", "wp"), None),
        P(("tile", "wp"), None),
        P(("tile", "wp")),
        P(),
    )
    out_specs = P("wp", "tile", None, None, None)
    return jax.shard_map(shards, mesh=mesh, in_specs=in_specs, out_specs=out_specs, check_vma=False)
```

```python
import functools

import jax
import jax.numpy as jnp
from jax import lax
from jax.experimental import pallas as pl
from jax.experimental.pallas import tpu as pltpu
from jax.sharding import PartitionSpec as P

TCOLS = 8
SUB = 64
KW = 8
OVER = 16
TILE = 1024
SIDE = TILE // SUB
PATCHES = SIDE * SIDE
EXT = SUB + KW
BLOCKS = 256
ZS, XS, YS, CORES = 8, 4, 4, 2
GROUP = 16
LINES = 3 * GROUP + 2
EARLY = 8
MESH = pl.DeviceIdType.MESH
bf16, f32, i32 = jnp.bfloat16, jnp.float32, jnp.int32


def position():
    tile, y = lax.axis_index("tile"), lax.axis_index("wp")
    return tile // (XS * CORES), (tile // CORES) % XS, tile % CORES, y


def offset(order, size):
    if isinstance(order, int):
        return size // 2 + (order // 2 if order % 2 == 0 else -((order + 1) // 2))
    return size // 2 + jnp.where(order % 2 == 0, order // 2, -((order + 1) // 2))


def far_step(step):
    return offset(step // 2, ZS), (step + 1) % 2


def near_step(step):
    return offset(step // 4, XS), offset(step % 4, YS)


def exchange_kernel(source_ref, patch_ref, vis_any, weight_any, cell_any, tap_any,
                    got_far, got_near, patches_ref,
                    vis_ref, weight_ref, cell_ref, tap_ref,
                    far_data, near_data, far_middle, near_middle, far_lines, near_lines,
                    far_marks, near_marks, load_sem, local,
                    far_out1, far_in1, near_out1, near_in1, far_out2, far_in2, near_out2, near_in2,
                    far_out3, far_in3, near_out3, near_in3):
    z, x, core, y = position()
    own = GROUP - 1

    loads = []
    for index, (source, target) in enumerate((
            (vis_any, vis_ref), (weight_any, weight_ref), (cell_any, cell_ref), (tap_any, tap_ref))):
        load = pltpu.make_async_copy(source, target.at[pl.ds(0, BLOCKS)], load_sem.at[index])
        load.start()
        loads.append(load)
        target[BLOCKS:] = jnp.zeros_like(target[BLOCKS:])

    def far_device(step):
        dz, dc = far_step(step)
        return ((((z + dz) % ZS) * XS + x) * CORES + (core + dc) % CORES, y)

    def near_device(step):
        dx, dy = near_step(step)
        return ((z * XS + (x + dx) % XS) * CORES + core, (y + dy) % YS)

    barrier = pltpu.get_barrier_semaphore()
    for step in range(own):
        pl.semaphore_signal(barrier, inc=1, device_id=far_device(step), device_id_type=MESH)
        pl.semaphore_signal(barrier, inc=1, device_id=near_device(step), device_id_type=MESH)
    for load in loads:
        load.wait()

    lane = lax.broadcasted_iota(i32, (1, 128), 1)

    def fill(data, slot, first):
        def line(number, carry):
            marks = jnp.zeros((1, 128), i32)
            for k in range(8):
                second = number * 8 + k
                block = source_ref[slot, first * GROUP + second if slot == 0 else second * GROUP + first]
                weight = weight_ref[pl.ds(block, 1), :]
                data[first, 3 * second] = vis_ref[block, 0:1, :] * weight
                data[first, 3 * second + 1] = vis_ref[block, 1:2, :] * weight
                code = cell_ref[pl.ds(block, 1), :] * (OVER * OVER) + tap_ref[pl.ds(block, 1), :]
                data[first, 3 * second + 2] = code.astype(f32)
                patch = patch_ref[jnp.minimum(block, BLOCKS - 1)]
                marks = jnp.where(lane == first + GROUP * k, patch, marks)
            data[first, 3 * GROUP + number] = marks.astype(f32)
            return carry

        lax.fori_loop(0, 2, line, 0)

    def send(source, target, out_sem, in_sem, index, device):
        copy = pltpu.make_async_remote_copy(
            src_ref=source, dst_ref=target, send_sem=out_sem.at[index], recv_sem=in_sem.at[index],
            device_id=device, device_id_type=MESH)
        copy.start()
        return copy

    def keep(source, target, index):
        copy = pltpu.make_async_copy(source, target, local.at[index])
        copy.start()
        return copy

    far_first, near_first = [], []
    for step in range(GROUP):
        fill(far_data, 0, step)
        if step == 0:
            pl.semaphore_wait(barrier, 2 * own)
        if step < own:
            far_first.append(send(far_data.at[step], far_middle.at[step], far_out1, far_in1, step, far_device(step)))
        else:
            far_first.append(keep(far_data.at[step], far_middle.at[step], 0))
        fill(near_data, 1, step)
        if step < own:
            near_first.append(send(near_data.at[step], near_middle.at[step], near_out1, near_in1, step, near_device(step)))
        else:
            near_first.append(keep(near_data.at[step], near_middle.at[step], 1))

    def arrive(copies, middle, lines):
        for copy in copies[:own]:
            copy.wait_recv()
        copies[own].wait()
        for line in range(2):
            total = middle[0, 3 * GROUP + line]
            for step in range(1, GROUP):
                total = total + middle[step, 3 * GROUP + line]
            lines[line] = total

    def far_second(step):
        part = near_middle.at[:, pl.ds(3 * step, 3)]
        line = near_lines.at[step // 8]
        if step == own:
            return [keep(part, got_near.at[step], 2), keep(line, near_marks.at[step], 3)]
        return [send(part, got_near.at[step], far_out2, far_in2, step, far_device(step)),
                send(line, near_marks.at[step], far_out3, far_in3, step, far_device(step))]

    def near_second(step):
        part = far_middle.at[:, pl.ds(3 * step, 3)]
        line = far_lines.at[step // 8]
        if step == own:
            return [keep(part, got_far.at[step], 4), keep(line, far_marks.at[step], 5)]
        return [send(part, got_far.at[step], near_out2, near_in2, step, near_device(step)),
                send(line, far_marks.at[step], near_out3, near_in3, step, near_device(step))]

    second = []
    arrive(near_first, near_middle, near_lines)
    for step in range(EARLY):
        second += far_second(step)
    arrive(far_first, far_middle, far_lines)
    for step in range(GROUP):
        second += near_second(step)
        if step + EARLY < GROUP:
            second += far_second(step + EARLY)
    for copy in second:
        copy.wait()
    for copy in far_first[:own] + near_first[:own]:
        copy.wait_send()
    for row, marks in ((0, far_marks), (2, near_marks)):
        for line in range(2):
            total = jnp.zeros((1, 128), f32)
            for k in range(8):
                total = jnp.where(lane // GROUP == k, marks[line * 8 + k], total)
            patches_ref[row + line:row + line + 1, :] = total.astype(i32)


def exchange(source, patch_index, visibilities, vis_weight, cell_index, tap_offsets):
    smem, hbm = pl.BlockSpec(memory_space=pltpu.SMEM), pl.BlockSpec(memory_space=pl.ANY)
    got = jax.ShapeDtypeStruct((GROUP, GROUP, 3, 1, 128), f32)
    message = pltpu.VMEM((GROUP, LINES, 1, 128), f32)
    return pl.pallas_call(
        exchange_kernel,
        out_shape=(got, got, jax.ShapeDtypeStruct((4, 128), i32)),
        in_specs=[smem, smem] + [hbm] * 4,
        out_specs=(hbm, hbm, pl.BlockSpec(memory_space=pltpu.VMEM)),
        scratch_shapes=[
            pltpu.VMEM((BLOCKS + 8, 2, 128), f32), pltpu.VMEM((BLOCKS + 8, 128), f32),
            pltpu.VMEM((BLOCKS + 8, 128), i32), pltpu.VMEM((BLOCKS + 8, 128), i32),
            message, message, message, message,
            pltpu.VMEM((2, 1, 128), f32), pltpu.VMEM((2, 1, 128), f32),
            pltpu.VMEM((GROUP, 1, 128), f32), pltpu.VMEM((GROUP, 1, 128), f32),
            pltpu.SemaphoreType.DMA((4,)), pltpu.SemaphoreType.DMA((6,)),
        ] + [pltpu.SemaphoreType.DMA((GROUP,))] * 12,
        compiler_params=pltpu.CompilerParams(
            collective_id=0, has_side_effects=True, vmem_limit_bytes=60 << 20),
    )(source, patch_index, visibilities, vis_weight, cell_index, tap_offsets)


UNROLL = 64
SLOTS = 2 * BLOCKS
ROWS = 2 * EXT
CHUNKS = 4


def halves(value):
    high = value.astype(bf16).astype(f32)
    rest = value - high
    return (jnp.concatenate([high, high], 0).astype(bf16), jnp.concatenate([rest, rest], 0).astype(bf16))


def contract(left, right):
    return lax.dot_general(left, right, (((1,), (1,)), ((), ())), preferred_element_type=f32)


def column(row):
    return jnp.transpose(jnp.broadcast_to(row, (128, 128)))


def grid_kernel(patch_ref, far_any, near_any, taps_ref, tile_ref, right_ref, lower_ref, corner_ref,
                total, got, stage, beyond, sorted_rows, sorted_keys, taps, load_sem, stage_sem):
    loads = []
    for slot, source in enumerate((far_any, near_any)):
        load = pltpu.make_async_copy(source, got.at[pl.ds(slot * BLOCKS, BLOCKS)], load_sem.at[slot])
        load.start()
        loads.append(load)

    lane = lax.broadcasted_iota(i32, (1, 128), 1)
    keys = [(patch_ref[c:c + 1, :] * SLOTS + (lane + 128 * c)).astype(f32) for c in range(4)]
    key_columns = [column(key) for key in keys]
    ranks = []
    for key in keys:
        below = [jnp.where(other < key, 1.0, 0.0) for other in key_columns]
        ranks.append(jnp.sum(below[0] + below[1] + below[2] + below[3], axis=0, keepdims=True))
    rank_columns = [column(rank) for rank in ranks]
    for c in range(4):
        place = (lane + 128 * c).astype(f32)
        here = [jnp.where(rank_columns[d] == place, key_columns[d], 0.0) for d in range(4)]
        chosen = jnp.sum(here[0] + here[1] + here[2] + here[3], axis=0, keepdims=True)
        sorted_rows[c:c + 1, :] = chosen.astype(i32)
    load = pltpu.make_async_copy(sorted_rows, sorted_keys, load_sem.at[2])
    load.start()
    loads.append(load)

    def clear(k, carry):
        total[pl.ds(k * 4, 4)] = jnp.zeros((4, ROWS, 128), f32)
        return carry

    lax.fori_loop(0, (PATCHES + SIDE) // 4, clear, 0)

    taps[...] = jnp.zeros_like(taps)
    taps[:, 0:OVER] = taps_ref[...]
    wide = lax.broadcasted_iota(i32, (8, 128), 1)
    spread = jnp.take_along_axis(taps[...], wide // KW, axis=1)
    own = lax.broadcasted_iota(i32, (8, 128), 0) == wide % KW
    table = jnp.broadcast_to(jnp.sum(jnp.where(own, spread, 0.0), axis=0, keepdims=True), (8, 128))

    for load in loads:
        load.wait()

    row8 = lax.broadcasted_iota(i32, (8, 128), 0)
    zero = jnp.zeros((16, 128), bf16)

    def steps(cell):
        step = (cell + 7 - row8) >> 3
        return jnp.concatenate([step, step - 1], 0).astype(jnp.int16)

    def one(key):
        block = key % SLOTS
        real = got[block, 0]
        imag = got[block, 1]
        code = jnp.broadcast_to(got[block, 2], (8, 128)).astype(i32)
        cell_u = code >> 14
        cell_v = (code >> 8) & (SUB - 1)
        ku = jnp.take_along_axis(table, ((code >> 1) & 0x78) + ((row8 - cell_u) & 7), axis=1)
        kv = jnp.take_along_axis(table, ((code << 3) & 0x78) + ((row8 - cell_v) & 7), axis=1)
        step_u, step_v = steps(cell_u), steps(cell_v)
        masks_u = [step_u == jnp.int16(2 * t) for t in range(5)]
        masks_v = [step_v == jnp.int16(2 * t) for t in range(5)]

        def rows_u(first, second):
            return jnp.concatenate(
                [jnp.where(mask, value, zero) for value in (first, second) for mask in masks_u], 0)

        def rows_v(value):
            return jnp.concatenate([jnp.where(mask, value, zero) for mask in masks_v], 0)

        v_high, v_rest = halves(kv)
        r_high, r_rest = halves(ku * real)
        i_high, i_rest = halves(ku * imag)
        v_high, v_rest = rows_v(v_high), rows_v(v_rest)
        u_high, u_rest = rows_u(r_high, i_high), rows_u(r_rest, i_rest)
        out = contract(jnp.concatenate([u_high, u_rest, u_high], 1),
                       jnp.concatenate([v_high, v_high, v_rest], 1))
        patch = key // SLOTS + SIDE
        total[patch, 0:EXT, 0:80] = total[patch, 0:EXT, 0:80] + out[0:EXT]
        total[patch, EXT:ROWS, 0:80] = total[patch, EXT:ROWS, 0:80] + out[80:80 + EXT]

    lane = lax.broadcasted_iota(i32, (8, 128), 1)

    def joined(load, put):
        before = jnp.zeros((8, 128), f32)
        for pair in range(SIDE // 2):
            moved = pltpu.roll(load(2 * pair + 1), SUB, 1)
            put(pair, load(2 * pair) + jnp.where(lane >= SUB, moved, before))
            before = moved
        return jnp.where(lane < KW, before, 0.0)

    def stripe(patch_row):
        for part in range(2):
            for step in range(SUB // 8):
                start = part * EXT + step * 8

                def load(column):
                    value = total[(patch_row + 1) * SIDE + column, start:start + 8, :]
                    if step == 0:
                        last = part * EXT + SUB
                        value = value + total[patch_row * SIDE + column, last:last + 8, :]
                    return value

                def put(pair, value):
                    place = pl.multiple_of(patch_row * SUB + step * 8, 8)
                    stage[part, pl.ds(place, 8), pair * 128:pair * 128 + 128] = value

                past = joined(load, put)
                beyond[patch_row, part, step * 8:step * 8 + 8, :] = past

    def each(patch_row, carry):
        stripe(patch_row)
        for part in range(2):
            for chunk in range(CHUNKS):
                rows = pl.ds(patch_row * SUB + chunk * (SUB // CHUNKS), SUB // CHUNKS)
                pltpu.make_async_copy(stage.at[part, rows], tile_ref.at[part, rows], stage_sem).start()
        return carry

    def key_at(position):
        return sorted_keys[position // 128, position % 128]

    def several(k, done):
        for q in range(UNROLL):
            one(key_at(k * UNROLL + q))
        following = key_at(jnp.minimum((k + 1) * UNROLL, SLOTS - 1)) // (SLOTS * SIDE)
        ready = jnp.where(k == SLOTS // UNROLL - 1, SIDE, following)
        lax.fori_loop(done, ready, each, 0)
        return ready

    lax.fori_loop(0, SLOTS // UNROLL, several, 0)

    for part in range(2):
        last = part * EXT + SUB

        def load(column):
            return total[SIDE * SIDE + column, last:last + 8, :]

        def put(pair, value):
            lower_ref[part, :, pair * 128:pair * 128 + 128] = value

        corner_ref[part] = joined(load, put)
    for part in range(2):
        for step in range(SUB // 8):
            rows = slice(step * 8, step * 8 + 8)
            packed = beyond[0, part, rows, :]
            for patch_row in range(1, SIDE):
                packed = packed + pltpu.roll(beyond[patch_row, part, rows, :], patch_row * KW, 1)
            right_ref[part, rows, :] = packed
    pltpu.make_async_copy(stage, tile_ref, stage_sem).wait()


def make_tile(patches, far, near, taps):
    vmem, hbm = pl.BlockSpec(memory_space=pltpu.VMEM), pl.BlockSpec(memory_space=pl.ANY)
    return pl.pallas_call(
        grid_kernel,
        out_shape=(
            jax.ShapeDtypeStruct((2, TILE, TILE), f32), jax.ShapeDtypeStruct((2, SUB, 128), f32),
            jax.ShapeDtypeStruct((2, KW, TILE), f32), jax.ShapeDtypeStruct((2, KW, 128), f32)),
        in_specs=[vmem, hbm, hbm, vmem],
        out_specs=(hbm, vmem, vmem, vmem),
        scratch_shapes=[
            pltpu.VMEM((PATCHES + SIDE, ROWS, 128), f32),
            pltpu.VMEM((SLOTS, 3, 1, 128), f32),
            pltpu.VMEM((2, TILE, TILE), f32),
            pltpu.VMEM((SIDE, 2, SUB, 128), f32),
            pltpu.VMEM((4, 128), i32), pltpu.SMEM((4, 128), i32), pltpu.VMEM((KW, 128), f32),
            pltpu.SemaphoreType.DMA((3,)), pltpu.SemaphoreType.DMA,
        ],
        compiler_params=pltpu.CompilerParams(vmem_limit_bytes=60 << 20),
    )(patches, far, near, taps)


def margins_kernel(right_ref, lower_ref, corner_ref, left_in, upper_in, corner_in, out_sem, in_sem):
    tile, y = lax.axis_index("tile"), lax.axis_index("wp")
    tiles = ZS * XS * CORES
    barrier = pltpu.get_barrier_semaphore()
    steps = (1, TCOLS, TCOLS + 1)
    for step in steps:
        for to in ((tile + step) % tiles, (tile + tiles - step) % tiles):
            pl.semaphore_signal(barrier, inc=1, device_id=(to, y), device_id_type=MESH)
    pl.semaphore_wait(barrier, 2 * len(steps))
    copies = []
    for index, (source, target) in enumerate(
            ((right_ref, left_in), (lower_ref, upper_in), (corner_ref, corner_in))):
        copy = pltpu.make_async_remote_copy(
            src_ref=source, dst_ref=target, send_sem=out_sem.at[index], recv_sem=in_sem.at[index],
            device_id=((tile + steps[index]) % tiles, y), device_id_type=MESH)
        copy.start()
        copies.append(copy)
    for copy in copies:
        copy.wait()


def margins(right, lower, corner):
    hbm = pl.BlockSpec(memory_space=pl.ANY)
    return pl.pallas_call(
        margins_kernel,
        out_shape=tuple(jax.ShapeDtypeStruct(a.shape, a.dtype) for a in (right, lower, corner)),
        in_specs=[hbm] * 3,
        out_specs=(hbm,) * 3,
        scratch_shapes=[pltpu.SemaphoreType.DMA((3,)), pltpu.SemaphoreType.DMA((3,))],
        compiler_params=pltpu.CompilerParams(collective_id=1, has_side_effects=True, vmem_limit_bytes=60 << 20),
    )(right, lower, corner)


def finish_kernel(tile_in, left_any, upper_any, corner_any, tile_ref,
                  side, top, left_in, upper_in, corner_in, sems):
    del tile_in
    tile = lax.axis_index("tile")
    has_left = jnp.where(tile % TCOLS > 0, 1.0, 0.0).astype(f32)
    has_upper = jnp.where(tile // TCOLS > 0, 1.0, 0.0).astype(f32)
    sides = tile_ref.at[:, :, pl.ds(0, 128)]
    tops = tile_ref.at[:, pl.ds(0, KW), pl.ds(128, TILE - 128)]
    read_side = pltpu.make_async_copy(sides, side, sems.at[0])
    read_top = pltpu.make_async_copy(tops, top, sems.at[1])
    read_side.start()
    read_top.start()
    loads = []
    for index, (source, target) in enumerate(
            ((upper_any, upper_in), (left_any, left_in), (corner_any, corner_in))):
        load = pltpu.make_async_copy(source, target, sems.at[2 + index])
        load.start()
        loads.append(load)
    lane = lax.broadcasted_iota(i32, (SUB, 128), 1)
    read_top.wait()
    loads[0].wait()
    top[...] = top[...] + upper_in[:, :, 128:] * has_upper
    write_top = pltpu.make_async_copy(top, tops, sems.at[1])
    write_top.start()
    read_side.wait()
    loads[1].wait()
    loads[2].wait()
    for part in range(2):
        packed = left_in[part] * has_left
        for patch_row in range(SIDE):
            rows = slice(patch_row * SUB, patch_row * SUB + SUB)
            moved = packed if patch_row == 0 else pltpu.roll(packed, 128 - KW * patch_row, 1)
            side[part, rows, :] = side[part, rows, :] + jnp.where(lane < KW, moved, 0.0)
        side[part, 0:KW, :] = (side[part, 0:KW, :] + upper_in[part, :, 0:128] * has_upper
                               + corner_in[part] * (has_left * has_upper))
    write_side = pltpu.make_async_copy(side, sides, sems.at[0])
    write_side.start()
    write_top.wait()
    write_side.wait()


def finish(tile, left, upper, corner):
    hbm = pl.BlockSpec(memory_space=pl.ANY)
    return pl.pallas_call(
        finish_kernel,
        out_shape=jax.ShapeDtypeStruct(tile.shape, tile.dtype),
        in_specs=[hbm] * 4,
        out_specs=hbm,
        scratch_shapes=[
            pltpu.VMEM((2, TILE, 128), f32), pltpu.VMEM((2, KW, TILE - 128), f32),
            pltpu.VMEM(left.shape, f32), pltpu.VMEM(upper.shape, f32), pltpu.VMEM(corner.shape, f32),
            pltpu.SemaphoreType.DMA((5,))],
        input_output_aliases={0: 0},
        compiler_params=pltpu.CompilerParams(vmem_limit_bytes=60 << 20),
    )(tile, left, upper, corner)


def shards(visibilities, vis_weight, cell_index, tap_offsets, routes, patch_index, kernel):
    blocks = visibilities.shape[0]
    block_ids = lax.broadcasted_iota(i32, (blocks, blocks), 0)
    step = lax.broadcasted_iota(i32, (blocks, blocks), 1)
    z, x, core, y = position()
    (dz, dc), (dx, dy) = far_step(step // GROUP), near_step(step % GROUP)
    target = ((((z + dz) % ZS) * XS + (x + dx) % XS) * CORES + (core + dc) % CORES) * YS + (y + dy) % YS
    named = routes == target
    first = jnp.min(jnp.where(named, block_ids, blocks), axis=0)
    last = jnp.max(jnp.where(named, block_ids, -1), axis=0)
    source = jnp.stack([first, jnp.where(last > first, last, blocks)])
    far, near, patches = exchange(source, patch_index, visibilities, vis_weight, cell_index, tap_offsets)
    tile, right, lower, corner = make_tile(
        patches, far.reshape(BLOCKS, 3, 1, 128), near.reshape(BLOCKS, 3, 1, 128), kernel.T)
    tile = finish(tile, *margins(right, lower, corner))
    return tile.reshape(1, 1, 2, TILE, TILE)


def solution(mesh):
    in_specs = (
        P(("tile", "wp"), None, None),
        P(("tile", "wp"), None),
        P(("tile", "wp"), None),
        P(("tile", "wp"), None),
        P(("tile", "wp"), None),
        P(("tile", "wp")),
        P(),
    )
    out_specs = P("wp", "tile", None, None, None)
    return jax.shard_map(shards, mesh=mesh, in_specs=in_specs, out_specs=out_specs, check_vma=False)
```

```python
import functools

import jax
import jax.numpy as jnp
from jax import lax
from jax.experimental import pallas as pl
from jax.experimental.pallas import tpu as pltpu
from jax.sharding import PartitionSpec as P

TCOLS = 8
SUB = 64
KW = 8
OVER = 16
TILE = 1024
SIDE = TILE // SUB
PATCHES = SIDE * SIDE
EXT = SUB + KW
BLOCKS = 256
ZS, XS, YS, CORES = 8, 4, 4, 2
GROUP = 16
LINES = 3 * GROUP + 2
EARLY = 8
MESH = pl.DeviceIdType.MESH
bf16, f32, i32 = jnp.bfloat16, jnp.float32, jnp.int32


def position():
    tile, y = lax.axis_index("tile"), lax.axis_index("wp")
    return tile // (XS * CORES), (tile // CORES) % XS, tile % CORES, y


def offset(order, size):
    if isinstance(order, int):
        return size // 2 + (order // 2 if order % 2 == 0 else -((order + 1) // 2))
    return size // 2 + jnp.where(order % 2 == 0, order // 2, -((order + 1) // 2))


def far_step(step):
    return offset(step // 2, ZS), (step + 1) % 2


def near_step(step):
    return offset(step // 4, XS), offset(step % 4, YS)


def exchange_kernel(patch_ref, routes_any, vis_any, weight_any, cell_any, tap_any,
                    got_far, got_near, patches_ref,
                    vis_ref, weight_ref, cell_ref, tap_ref, routes_ref, source_rows, source_ref,
                    far_data, near_data, far_middle, near_middle, far_lines, near_lines,
                    far_marks, near_marks, load_sem, local,
                    far_out1, far_in1, near_out1, near_in1, far_out2, far_in2, near_out2, near_in2,
                    far_out3, far_in3, near_out3, near_in3):
    z, x, core, y = position()
    own = GROUP - 1

    loads = []
    for index, (source, target) in enumerate((
            (vis_any, vis_ref), (weight_any, weight_ref), (cell_any, cell_ref), (tap_any, tap_ref))):
        load = pltpu.make_async_copy(source, target.at[pl.ds(0, BLOCKS)], load_sem.at[index])
        load.start()
        loads.append(load)
        target[BLOCKS:] = jnp.zeros_like(target[BLOCKS:])

    route_load = pltpu.make_async_copy(routes_any, routes_ref, load_sem.at[4])
    route_load.start()

    def far_device(step):
        dz, dc = far_step(step)
        return ((((z + dz) % ZS) * XS + x) * CORES + (core + dc) % CORES, y)

    def near_device(step):
        dx, dy = near_step(step)
        return ((z * XS + (x + dx) % XS) * CORES + core, (y + dy) % YS)

    barrier = pltpu.get_barrier_semaphore()
    for step in range(own):
        pl.semaphore_signal(barrier, inc=1, device_id=far_device(step), device_id_type=MESH)
        pl.semaphore_signal(barrier, inc=1, device_id=near_device(step), device_id_type=MESH)
    lane = lax.broadcasted_iota(i32, (1, 128), 1)
    route_load.wait()
    row = lax.broadcasted_iota(i32, (128, 128), 0)
    columns = [jnp.transpose(jnp.broadcast_to(routes_ref[:, 128 * d:128 * d + 128], (128, 128))) for d in range(2)]

    def ring(order, size):
        return size // 2 + jnp.where(order & 1 == 0, order >> 1, -((order + 1) >> 1))

    for c in range(2):
        step = lane + 128 * c
        far, near = step >> 4, step & (GROUP - 1)
        to_z, to_core = (z + ring(far >> 1, ZS)) & (ZS - 1), (core + far + 1) & (CORES - 1)
        to_x, to_y = (x + ring(near >> 2, XS)) & (XS - 1), (y + ring(near & (YS - 1), YS)) & (YS - 1)
        target = ((to_z * XS + to_x) * CORES + to_core) * YS + to_y
        named = [column == target for column in columns]
        first = jnp.minimum(jnp.where(named[0], row, BLOCKS), jnp.where(named[1], row + 128, BLOCKS))
        last = jnp.maximum(jnp.where(named[0], row, -1), jnp.where(named[1], row + 128, -1))
        first, last = jnp.min(first, axis=0, keepdims=True), jnp.max(last, axis=0, keepdims=True)
        source_rows[c:c + 1, :] = first
        source_rows[2 + c:3 + c, :] = jnp.where(last > first, last, BLOCKS)
    numbers = pltpu.make_async_copy(source_rows, source_ref, load_sem.at[5])
    numbers.start()
    for load in loads:
        load.wait()
    numbers.wait()

    def fill(data, slot, first):
        def line(number, carry):
            marks = jnp.zeros((1, 128), i32)
            for k in range(8):
                second = number * 8 + k
                step = first * GROUP + second if slot == 0 else second * GROUP + first
                block = source_ref[2 * slot + step // 128, step % 128]
                weight = weight_ref[pl.ds(block, 1), :]
                data[first, 3 * second] = vis_ref[block, 0:1, :] * weight
                data[first, 3 * second + 1] = vis_ref[block, 1:2, :] * weight
                code = cell_ref[pl.ds(block, 1), :] * (OVER * OVER) + tap_ref[pl.ds(block, 1), :]
                data[first, 3 * second + 2] = code.astype(f32)
                patch = patch_ref[jnp.minimum(block, BLOCKS - 1)]
                marks = jnp.where(lane == first + GROUP * k, patch, marks)
            data[first, 3 * GROUP + number] = marks.astype(f32)
            return carry

        lax.fori_loop(0, 2, line, 0)

    def send(source, target, out_sem, in_sem, index, device):
        copy = pltpu.make_async_remote_copy(
            src_ref=source, dst_ref=target, send_sem=out_sem.at[index], recv_sem=in_sem.at[index],
            device_id=device, device_id_type=MESH)
        copy.start()
        return copy

    def keep(source, target, index):
        copy = pltpu.make_async_copy(source, target, local.at[index])
        copy.start()
        return copy

    far_first, near_first = [], []
    for step in range(GROUP):
        fill(far_data, 0, step)
        if step == 0:
            pl.semaphore_wait(barrier, 2 * own)
        if step < own:
            far_first.append(send(far_data.at[step], far_middle.at[step], far_out1, far_in1, step, far_device(step)))
        else:
            far_first.append(keep(far_data.at[step], far_middle.at[step], 0))
        fill(near_data, 1, step)
        if step < own:
            near_first.append(send(near_data.at[step], near_middle.at[step], near_out1, near_in1, step, near_device(step)))
        else:
            near_first.append(keep(near_data.at[step], near_middle.at[step], 1))

    def arrive(copies, middle, lines):
        for copy in copies[:own]:
            copy.wait_recv()
        copies[own].wait()
        for line in range(2):
            total = middle[0, 3 * GROUP + line]
            for step in range(1, GROUP):
                total = total + middle[step, 3 * GROUP + line]
            lines[line] = total

    def far_second(step):
        part = near_middle.at[:, pl.ds(3 * step, 3)]
        line = near_lines.at[step // 8]
        if step == own:
            return [keep(part, got_near.at[step], 2), keep(line, near_marks.at[step], 3)]
        return [send(part, got_near.at[step], far_out2, far_in2, step, far_device(step)),
                send(line, near_marks.at[step], far_out3, far_in3, step, far_device(step))]

    def near_second(step):
        part = far_middle.at[:, pl.ds(3 * step, 3)]
        line = far_lines.at[step // 8]
        if step == own:
            return [keep(part, got_far.at[step], 4), keep(line, far_marks.at[step], 5)]
        return [send(part, got_far.at[step], near_out2, near_in2, step, near_device(step)),
                send(line, far_marks.at[step], near_out3, near_in3, step, near_device(step))]

    second = []
    arrive(near_first, near_middle, near_lines)
    for step in range(EARLY):
        second += far_second(step)
    arrive(far_first, far_middle, far_lines)
    for step in range(GROUP):
        second += near_second(step)
        if step + EARLY < GROUP:
            second += far_second(step + EARLY)
    for copy in second:
        copy.wait()
    for copy in far_first[:own] + near_first[:own]:
        copy.wait_send()
    for row, marks in ((0, far_marks), (2, near_marks)):
        for line in range(2):
            total = jnp.zeros((1, 128), f32)
            for k in range(8):
                total = jnp.where(lane // GROUP == k, marks[line * 8 + k], total)
            patches_ref[row + line:row + line + 1, :] = total.astype(i32)


def exchange(patch_index, routes, visibilities, vis_weight, cell_index, tap_offsets):
    smem, hbm = pl.BlockSpec(memory_space=pltpu.SMEM), pl.BlockSpec(memory_space=pl.ANY)
    got = jax.ShapeDtypeStruct((GROUP, GROUP, 3, 1, 128), f32)
    message = pltpu.VMEM((GROUP, LINES, 1, 128), f32)
    return pl.pallas_call(
        exchange_kernel,
        out_shape=(got, got, jax.ShapeDtypeStruct((4, 128), i32)),
        in_specs=[smem] + [hbm] * 5,
        out_specs=(hbm, hbm, pl.BlockSpec(memory_space=pltpu.VMEM)),
        scratch_shapes=[
            pltpu.VMEM((BLOCKS + 8, 2, 128), f32), pltpu.VMEM((BLOCKS + 8, 128), f32),
            pltpu.VMEM((BLOCKS + 8, 128), i32), pltpu.VMEM((BLOCKS + 8, 128), i32),
            pltpu.VMEM((1, BLOCKS), i32), pltpu.VMEM((4, 128), i32), pltpu.SMEM((4, 128), i32),
            message, message, message, message,
            pltpu.VMEM((2, 1, 128), f32), pltpu.VMEM((2, 1, 128), f32),
            pltpu.VMEM((GROUP, 1, 128), f32), pltpu.VMEM((GROUP, 1, 128), f32),
            pltpu.SemaphoreType.DMA((6,)), pltpu.SemaphoreType.DMA((6,)),
        ] + [pltpu.SemaphoreType.DMA((GROUP,))] * 12,
        compiler_params=pltpu.CompilerParams(
            collective_id=0, has_side_effects=True, vmem_limit_bytes=60 << 20),
    )(patch_index, routes, visibilities, vis_weight, cell_index, tap_offsets)


UNROLL = 64
SLOTS = 2 * BLOCKS
ROWS = 2 * EXT
CHUNKS = 4


def halves(value):
    high = value.astype(bf16).astype(f32)
    rest = value - high
    return (jnp.concatenate([high, high], 0).astype(bf16), jnp.concatenate([rest, rest], 0).astype(bf16))


def contract(left, right):
    return lax.dot_general(left, right, (((1,), (1,)), ((), ())), preferred_element_type=f32)


def column(row):
    return jnp.transpose(jnp.broadcast_to(row, (128, 128)))


def grid_kernel(patch_ref, far_any, near_any, taps_ref, tile_ref, right_ref, lower_ref, corner_ref,
                total, got, stage, beyond, sorted_rows, sorted_keys, taps, load_sem, stage_sem):
    loads = []
    for slot, source in enumerate((far_any, near_any)):
        load = pltpu.make_async_copy(source, got.at[pl.ds(slot * BLOCKS, BLOCKS)], load_sem.at[slot])
        load.start()
        loads.append(load)

    lane = lax.broadcasted_iota(i32, (1, 128), 1)
    keys = [(patch_ref[c:c + 1, :] * SLOTS + (lane + 128 * c)).astype(f32) for c in range(4)]
    key_columns = [column(key) for key in keys]
    ranks = []
    for key in keys:
        below = [jnp.where(other < key, 1.0, 0.0) for other in key_columns]
        ranks.append(jnp.sum(below[0] + below[1] + below[2] + below[3], axis=0, keepdims=True))
    rank_columns = [column(rank) for rank in ranks]
    for c in range(4):
        place = (lane + 128 * c).astype(f32)
        here = [jnp.where(rank_columns[d] == place, key_columns[d], 0.0) for d in range(4)]
        chosen = jnp.sum(here[0] + here[1] + here[2] + here[3], axis=0, keepdims=True)
        sorted_rows[c:c + 1, :] = chosen.astype(i32)
    load = pltpu.make_async_copy(sorted_rows, sorted_keys, load_sem.at[2])
    load.start()
    loads.append(load)

    def clear(k, carry):
        total[pl.ds(k * 4, 4)] = jnp.zeros((4, ROWS, 128), f32)
        return carry

    lax.fori_loop(0, (PATCHES + SIDE) // 4, clear, 0)

    taps[...] = jnp.zeros_like(taps)
    taps[:, 0:OVER] = taps_ref[...]
    wide = lax.broadcasted_iota(i32, (8, 128), 1)
    spread = jnp.take_along_axis(taps[...], wide // KW, axis=1)
    own = lax.broadcasted_iota(i32, (8, 128), 0) == wide % KW
    table = jnp.broadcast_to(jnp.sum(jnp.where(own, spread, 0.0), axis=0, keepdims=True), (8, 128))

    for load in loads:
        load.wait()

    row8 = lax.broadcasted_iota(i32, (8, 128), 0)
    zero = jnp.zeros((16, 128), bf16)

    def steps(cell):
        step = (cell + 7 - row8) >> 3
        return jnp.concatenate([step, step - 1], 0).astype(jnp.int16)

    def one(key):
        block = key % SLOTS
        real = got[block, 0]
        imag = got[block, 1]
        code = jnp.broadcast_to(got[block, 2], (8, 128)).astype(i32)
        cell_u = code >> 14
        cell_v = (code >> 8) & (SUB - 1)
        ku = jnp.take_along_axis(table, ((code >> 1) & 0x78) + ((row8 - cell_u) & 7), axis=1)
        kv = jnp.take_along_axis(table, ((code << 3) & 0x78) + ((row8 - cell_v) & 7), axis=1)
        step_u, step_v = steps(cell_u), steps(cell_v)
        masks_u = [step_u == jnp.int16(2 * t) for t in range(5)]
        masks_v = [step_v == jnp.int16(2 * t) for t in range(5)]

        def rows_u(first, second):
            return jnp.concatenate(
                [jnp.where(mask, value, zero) for value in (first, second) for mask in masks_u], 0)

        def rows_v(value):
            return jnp.concatenate([jnp.where(mask, value, zero) for mask in masks_v], 0)

        v_high, v_rest = halves(kv)
        r_high, r_rest = halves(ku * real)
        i_high, i_rest = halves(ku * imag)
        v_high, v_rest = rows_v(v_high), rows_v(v_rest)
        u_high, u_rest = rows_u(r_high, i_high), rows_u(r_rest, i_rest)
        out = contract(jnp.concatenate([u_high, u_rest, u_high], 1),
                       jnp.concatenate([v_high, v_high, v_rest], 1))
        patch = key // SLOTS + SIDE
        total[patch, 0:EXT, 0:80] = total[patch, 0:EXT, 0:80] + out[0:EXT]
        total[patch, EXT:ROWS, 0:80] = total[patch, EXT:ROWS, 0:80] + out[80:80 + EXT]

    lane = lax.broadcasted_iota(i32, (8, 128), 1)

    def joined(load, put):
        before = jnp.zeros((8, 128), f32)
        for pair in range(SIDE // 2):
            moved = pltpu.roll(load(2 * pair + 1), SUB, 1)
            put(pair, load(2 * pair) + jnp.where(lane >= SUB, moved, before))
            before = moved
        return jnp.where(lane < KW, before, 0.0)

    def stripe(patch_row):
        for part in range(2):
            for step in range(SUB // 8):
                start = part * EXT + step * 8

                def load(column):
                    value = total[(patch_row + 1) * SIDE + column, start:start + 8, :]
                    if step == 0:
                        last = part * EXT + SUB
                        value = value + total[patch_row * SIDE + column, last:last + 8, :]
                    return value

                def put(pair, value):
                    place = pl.multiple_of(patch_row * SUB + step * 8, 8)
                    stage[part, pl.ds(place, 8), pair * 128:pair * 128 + 128] = value

                past = joined(load, put)
                beyond[patch_row, part, step * 8:step * 8 + 8, :] = past

    def each(patch_row, carry):
        stripe(patch_row)
        for part in range(2):
            for chunk in range(CHUNKS):
                rows = pl.ds(patch_row * SUB + chunk * (SUB // CHUNKS), SUB // CHUNKS)
                pltpu.make_async_copy(stage.at[part, rows], tile_ref.at[part, rows], stage_sem).start()
        return carry

    def key_at(position):
        return sorted_keys[position // 128, position % 128]

    def several(k, done):
        for q in range(UNROLL):
            one(key_at(k * UNROLL + q))
        following = key_at(jnp.minimum((k + 1) * UNROLL, SLOTS - 1)) // (SLOTS * SIDE)
        ready = jnp.where(k == SLOTS // UNROLL - 1, SIDE, following)
        lax.fori_loop(done, ready, each, 0)
        return ready

    lax.fori_loop(0, SLOTS // UNROLL, several, 0)

    for part in range(2):
        last = part * EXT + SUB

        def load(column):
            return total[SIDE * SIDE + column, last:last + 8, :]

        def put(pair, value):
            lower_ref[part, :, pair * 128:pair * 128 + 128] = value

        corner_ref[part] = joined(load, put)
    for part in range(2):
        for step in range(SUB // 8):
            rows = slice(step * 8, step * 8 + 8)
            packed = beyond[0, part, rows, :]
            for patch_row in range(1, SIDE):
                packed = packed + pltpu.roll(beyond[patch_row, part, rows, :], patch_row * KW, 1)
            right_ref[part, rows, :] = packed
    pltpu.make_async_copy(stage, tile_ref, stage_sem).wait()


def make_tile(patches, far, near, taps):
    vmem, hbm = pl.BlockSpec(memory_space=pltpu.VMEM), pl.BlockSpec(memory_space=pl.ANY)
    return pl.pallas_call(
        grid_kernel,
        out_shape=(
            jax.ShapeDtypeStruct((2, TILE, TILE), f32), jax.ShapeDtypeStruct((2, SUB, 128), f32),
            jax.ShapeDtypeStruct((2, KW, TILE), f32), jax.ShapeDtypeStruct((2, KW, 128), f32)),
        in_specs=[vmem, hbm, hbm, vmem],
        out_specs=(hbm, vmem, vmem, vmem),
        scratch_shapes=[
            pltpu.VMEM((PATCHES + SIDE, ROWS, 128), f32),
            pltpu.VMEM((SLOTS, 3, 1, 128), f32),
            pltpu.VMEM((2, TILE, TILE), f32),
            pltpu.VMEM((SIDE, 2, SUB, 128), f32),
            pltpu.VMEM((4, 128), i32), pltpu.SMEM((4, 128), i32), pltpu.VMEM((KW, 128), f32),
            pltpu.SemaphoreType.DMA((3,)), pltpu.SemaphoreType.DMA,
        ],
        compiler_params=pltpu.CompilerParams(vmem_limit_bytes=60 << 20),
    )(patches, far, near, taps)


def margins_kernel(right_ref, lower_ref, corner_ref, left_in, upper_in, corner_in, out_sem, in_sem):
    tile, y = lax.axis_index("tile"), lax.axis_index("wp")
    tiles = ZS * XS * CORES
    barrier = pltpu.get_barrier_semaphore()
    steps = (1, TCOLS, TCOLS + 1)
    for step in steps:
        for to in ((tile + step) % tiles, (tile + tiles - step) % tiles):
            pl.semaphore_signal(barrier, inc=1, device_id=(to, y), device_id_type=MESH)
    pl.semaphore_wait(barrier, 2 * len(steps))
    copies = []
    for index, (source, target) in enumerate(
            ((right_ref, left_in), (lower_ref, upper_in), (corner_ref, corner_in))):
        copy = pltpu.make_async_remote_copy(
            src_ref=source, dst_ref=target, send_sem=out_sem.at[index], recv_sem=in_sem.at[index],
            device_id=((tile + steps[index]) % tiles, y), device_id_type=MESH)
        copy.start()
        copies.append(copy)
    for copy in copies:
        copy.wait()


def margins(right, lower, corner):
    hbm = pl.BlockSpec(memory_space=pl.ANY)
    return pl.pallas_call(
        margins_kernel,
        out_shape=tuple(jax.ShapeDtypeStruct(a.shape, a.dtype) for a in (right, lower, corner)),
        in_specs=[hbm] * 3,
        out_specs=(hbm,) * 3,
        scratch_shapes=[pltpu.SemaphoreType.DMA((3,)), pltpu.SemaphoreType.DMA((3,))],
        compiler_params=pltpu.CompilerParams(collective_id=1, has_side_effects=True, vmem_limit_bytes=60 << 20),
    )(right, lower, corner)


def finish_kernel(tile_in, left_any, upper_any, corner_any, tile_ref,
                  side, top, left_in, upper_in, corner_in, sems):
    del tile_in
    tile = lax.axis_index("tile")
    has_left = jnp.where(tile % TCOLS > 0, 1.0, 0.0).astype(f32)
    has_upper = jnp.where(tile // TCOLS > 0, 1.0, 0.0).astype(f32)
    sides = tile_ref.at[:, :, pl.ds(0, 128)]
    tops = tile_ref.at[:, pl.ds(0, KW), pl.ds(128, TILE - 128)]
    read_side = pltpu.make_async_copy(sides, side, sems.at[0])
    read_top = pltpu.make_async_copy(tops, top, sems.at[1])
    read_side.start()
    read_top.start()
    loads = []
    for index, (source, target) in enumerate(
            ((upper_any, upper_in), (left_any, left_in), (corner_any, corner_in))):
        load = pltpu.make_async_copy(source, target, sems.at[2 + index])
        load.start()
        loads.append(load)
    lane = lax.broadcasted_iota(i32, (SUB, 128), 1)
    read_top.wait()
    loads[0].wait()
    top[...] = top[...] + upper_in[:, :, 128:] * has_upper
    write_top = pltpu.make_async_copy(top, tops, sems.at[1])
    write_top.start()
    read_side.wait()
    loads[1].wait()
    loads[2].wait()
    for part in range(2):
        packed = left_in[part] * has_left
        for patch_row in range(SIDE):
            rows = slice(patch_row * SUB, patch_row * SUB + SUB)
            moved = packed if patch_row == 0 else pltpu.roll(packed, 128 - KW * patch_row, 1)
            side[part, rows, :] = side[part, rows, :] + jnp.where(lane < KW, moved, 0.0)
        side[part, 0:KW, :] = (side[part, 0:KW, :] + upper_in[part, :, 0:128] * has_upper
                               + corner_in[part] * (has_left * has_upper))
    write_side = pltpu.make_async_copy(side, sides, sems.at[0])
    write_side.start()
    write_top.wait()
    write_side.wait()


def finish(tile, left, upper, corner):
    hbm = pl.BlockSpec(memory_space=pl.ANY)
    return pl.pallas_call(
        finish_kernel,
        out_shape=jax.ShapeDtypeStruct(tile.shape, tile.dtype),
        in_specs=[hbm] * 4,
        out_specs=hbm,
        scratch_shapes=[
            pltpu.VMEM((2, TILE, 128), f32), pltpu.VMEM((2, KW, TILE - 128), f32),
            pltpu.VMEM(left.shape, f32), pltpu.VMEM(upper.shape, f32), pltpu.VMEM(corner.shape, f32),
            pltpu.SemaphoreType.DMA((5,))],
        input_output_aliases={0: 0},
        compiler_params=pltpu.CompilerParams(vmem_limit_bytes=60 << 20),
    )(tile, left, upper, corner)


def shards(visibilities, vis_weight, cell_index, tap_offsets, routes, patch_index, kernel):
    far, near, patches = exchange(
        patch_index, routes.reshape(1, BLOCKS), visibilities, vis_weight, cell_index, tap_offsets)
    tile, right, lower, corner = make_tile(
        patches, far.reshape(BLOCKS, 3, 1, 128), near.reshape(BLOCKS, 3, 1, 128), kernel.T)
    tile = finish(tile, *margins(right, lower, corner))
    return tile.reshape(1, 1, 2, TILE, TILE)


def solution(mesh):
    in_specs = (
        P(("tile", "wp"), None, None),
        P(("tile", "wp"), None),
        P(("tile", "wp"), None),
        P(("tile", "wp"), None),
        P(("tile", "wp"), None),
        P(("tile", "wp")),
        P(),
    )
    out_specs = P("wp", "tile", None, None, None)
    return jax.shard_map(shards, mesh=mesh, in_specs=in_specs, out_specs=out_specs, check_vma=False)
```

```python
import functools

import jax
import jax.numpy as jnp
from jax import lax
from jax.experimental import pallas as pl
from jax.experimental.pallas import tpu as pltpu
from jax.sharding import PartitionSpec as P

TCOLS = 8
SUB = 64
KW = 8
OVER = 16
TILE = 1024
SIDE = TILE // SUB
PATCHES = SIDE * SIDE
EXT = SUB + KW
BLOCKS = 256
ZS, XS, YS, CORES = 8, 4, 4, 2
GROUP = 16
LINES = 3 * GROUP + 2
EARLY = 8
MESH = pl.DeviceIdType.MESH
bf16, f32, i32 = jnp.bfloat16, jnp.float32, jnp.int32


def position():
    tile, y = lax.axis_index("tile"), lax.axis_index("wp")
    return tile // (XS * CORES), (tile // CORES) % XS, tile % CORES, y


def offset(order, size):
    if isinstance(order, int):
        return size // 2 + (order // 2 if order % 2 == 0 else -((order + 1) // 2))
    return size // 2 + jnp.where(order % 2 == 0, order // 2, -((order + 1) // 2))


def far_step(step):
    return offset(step // 2, ZS), (step + 1) % 2


def near_step(step):
    return offset(step // 4, XS), offset(step % 4, YS)


def exchange_kernel(patch_ref, routes_any, vis_any, weight_any, cell_any, tap_any,
                    got_far, got_near, patches_ref,
                    vis_ref, weight_ref, cell_ref, tap_ref, routes_ref, source_rows, source_ref,
                    far_data, near_data, far_middle, near_middle, far_lines, near_lines,
                    far_marks, near_marks, load_sem, local,
                    far_out1, far_in1, near_out1, near_in1, far_out2, far_in2, near_out2, near_in2,
                    far_out3, far_in3, near_out3, near_in3):
    z, x, core, y = position()
    own = GROUP - 1

    loads = []
    for index, (source, target) in enumerate((
            (vis_any, vis_ref), (weight_any, weight_ref), (cell_any, cell_ref), (tap_any, tap_ref))):
        load = pltpu.make_async_copy(source, target.at[pl.ds(0, BLOCKS)], load_sem.at[index])
        load.start()
        loads.append(load)
        target[BLOCKS:] = jnp.zeros_like(target[BLOCKS:])

    route_load = pltpu.make_async_copy(routes_any, routes_ref, load_sem.at[4])
    route_load.start()

    def far_device(step):
        dz, dc = far_step(step)
        return ((((z + dz) % ZS) * XS + x) * CORES + (core + dc) % CORES, y)

    def near_device(step):
        dx, dy = near_step(step)
        return ((z * XS + (x + dx) % XS) * CORES + core, (y + dy) % YS)

    barrier = pltpu.get_barrier_semaphore()
    for step in range(own):
        pl.semaphore_signal(barrier, inc=1, device_id=far_device(step), device_id_type=MESH)
        pl.semaphore_signal(barrier, inc=1, device_id=near_device(step), device_id_type=MESH)
    lane = lax.broadcasted_iota(i32, (1, 128), 1)
    route_load.wait()
    row = lax.broadcasted_iota(i32, (128, 128), 0)
    columns = [jnp.transpose(jnp.broadcast_to(routes_ref[:, 128 * d:128 * d + 128], (128, 128))) for d in range(2)]

    def ring(order, size):
        return size // 2 + jnp.where(order & 1 == 0, order >> 1, -((order + 1) >> 1))

    for c in range(2):
        step = lane + 128 * c
        far, near = step >> 4, step & (GROUP - 1)
        to_z, to_core = (z + ring(far >> 1, ZS)) & (ZS - 1), (core + far + 1) & (CORES - 1)
        to_x, to_y = (x + ring(near >> 2, XS)) & (XS - 1), (y + ring(near & (YS - 1), YS)) & (YS - 1)
        target = ((to_z * XS + to_x) * CORES + to_core) * YS + to_y
        named = [column == target for column in columns]
        first = jnp.minimum(jnp.where(named[0], row, BLOCKS), jnp.where(named[1], row + 128, BLOCKS))
        last = jnp.maximum(jnp.where(named[0], row, -1), jnp.where(named[1], row + 128, -1))
        first, last = jnp.min(first, axis=0, keepdims=True), jnp.max(last, axis=0, keepdims=True)
        source_rows[c:c + 1, :] = first
        source_rows[2 + c:3 + c, :] = jnp.where(last > first, last, BLOCKS)
    numbers = pltpu.make_async_copy(source_rows, source_ref, load_sem.at[5])
    numbers.start()
    for load in loads:
        load.wait()
    numbers.wait()

    def fill(data, slot, first):
        def line(number, carry):
            marks = jnp.zeros((1, 128), i32)
            for k in range(8):
                second = number * 8 + k
                step = first * GROUP + second if slot == 0 else second * GROUP + first
                block = source_ref[2 * slot + step // 128, step % 128]
                weight = weight_ref[pl.ds(block, 1), :]
                data[first, 3 * second] = vis_ref[block, 0:1, :] * weight
                data[first, 3 * second + 1] = vis_ref[block, 1:2, :] * weight
                code = cell_ref[pl.ds(block, 1), :] * (OVER * OVER) + tap_ref[pl.ds(block, 1), :]
                data[first, 3 * second + 2] = code.astype(f32)
                patch = patch_ref[jnp.minimum(block, BLOCKS - 1)]
                marks = jnp.where(lane == first + GROUP * k, patch, marks)
            data[first, 3 * GROUP + number] = marks.astype(f32)
            return carry

        lax.fori_loop(0, 2, line, 0)

    def send(source, target, out_sem, in_sem, index, device):
        copy = pltpu.make_async_remote_copy(
            src_ref=source, dst_ref=target, send_sem=out_sem.at[index], recv_sem=in_sem.at[index],
            device_id=device, device_id_type=MESH)
        copy.start()
        return copy

    def keep(source, target, index):
        copy = pltpu.make_async_copy(source, target, local.at[index])
        copy.start()
        return copy

    far_first, near_first = [], []
    for step in range(GROUP):
        fill(far_data, 0, step)
        if step == 0:
            pl.semaphore_wait(barrier, 2 * own)
        if step < own:
            far_first.append(send(far_data.at[step], far_middle.at[step], far_out1, far_in1, step, far_device(step)))
        else:
            far_first.append(keep(far_data.at[step], far_middle.at[step], 0))
        fill(near_data, 1, step)
        if step < own:
            near_first.append(send(near_data.at[step], near_middle.at[step], near_out1, near_in1, step, near_device(step)))
        else:
            near_first.append(keep(near_data.at[step], near_middle.at[step], 1))

    def arrive(copies, middle, lines):
        for copy in copies[:own]:
            copy.wait_recv()
        copies[own].wait()
        for line in range(2):
            total = middle[0, 3 * GROUP + line]
            for step in range(1, GROUP):
                total = total + middle[step, 3 * GROUP + line]
            lines[line] = total

    def far_second(step):
        part = near_middle.at[:, pl.ds(3 * step, 3)]
        line = near_lines.at[step // 8]
        if step == own:
            return [keep(part, got_near.at[step], 2), keep(line, near_marks.at[step], 3)]
        return [send(part, got_near.at[step], far_out2, far_in2, step, far_device(step)),
                send(line, near_marks.at[step], far_out3, far_in3, step, far_device(step))]

    def near_second(step):
        part = far_middle.at[:, pl.ds(3 * step, 3)]
        line = far_lines.at[step // 8]
        if step == own:
            return [keep(part, got_far.at[step], 4), keep(line, far_marks.at[step], 5)]
        return [send(part, got_far.at[step], near_out2, near_in2, step, near_device(step)),
                send(line, far_marks.at[step], near_out3, near_in3, step, near_device(step))]

    second = []
    arrive(near_first, near_middle, near_lines)
    for step in range(EARLY):
        second += far_second(step)
    arrive(far_first, far_middle, far_lines)
    for step in range(GROUP):
        second += near_second(step)
        if step + EARLY < GROUP:
            second += far_second(step + EARLY)
    for copy in second:
        copy.wait()
    for copy in far_first[:own] + near_first[:own]:
        copy.wait_send()
    for row, marks in ((0, far_marks), (2, near_marks)):
        for line in range(2):
            total = jnp.zeros((1, 128), f32)
            for k in range(8):
                total = jnp.where(lane // GROUP == k, marks[line * 8 + k], total)
            patches_ref[row + line:row + line + 1, :] = total.astype(i32)


def exchange(patch_index, routes, visibilities, vis_weight, cell_index, tap_offsets):
    smem, hbm = pl.BlockSpec(memory_space=pltpu.SMEM), pl.BlockSpec(memory_space=pl.ANY)
    got = jax.ShapeDtypeStruct((GROUP, GROUP, 3, 1, 128), f32)
    message = pltpu.VMEM((GROUP, LINES, 1, 128), f32)
    return pl.pallas_call(
        exchange_kernel,
        out_shape=(got, got, jax.ShapeDtypeStruct((4, 128), i32)),
        in_specs=[smem] + [hbm] * 5,
        out_specs=(hbm, hbm, pl.BlockSpec(memory_space=pltpu.VMEM)),
        scratch_shapes=[
            pltpu.VMEM((BLOCKS + 8, 2, 128), f32), pltpu.VMEM((BLOCKS + 8, 128), f32),
            pltpu.VMEM((BLOCKS + 8, 128), i32), pltpu.VMEM((BLOCKS + 8, 128), i32),
            pltpu.VMEM((1, BLOCKS), i32), pltpu.VMEM((4, 128), i32), pltpu.SMEM((4, 128), i32),
            message, message, message, message,
            pltpu.VMEM((2, 1, 128), f32), pltpu.VMEM((2, 1, 128), f32),
            pltpu.VMEM((GROUP, 1, 128), f32), pltpu.VMEM((GROUP, 1, 128), f32),
            pltpu.SemaphoreType.DMA((6,)), pltpu.SemaphoreType.DMA((6,)),
        ] + [pltpu.SemaphoreType.DMA((GROUP,))] * 12,
        compiler_params=pltpu.CompilerParams(
            collective_id=0, has_side_effects=True, vmem_limit_bytes=60 << 20),
    )(patch_index, routes, visibilities, vis_weight, cell_index, tap_offsets)


UNROLL = 128
SLOTS = 2 * BLOCKS
ROWS = 2 * EXT
CHUNKS = 4


def halves(value):
    high = value.astype(bf16).astype(f32)
    rest = value - high
    return (jnp.concatenate([high, high], 0).astype(bf16), jnp.concatenate([rest, rest], 0).astype(bf16))


def contract(left, right):
    return lax.dot_general(left, right, (((1,), (1,)), ((), ())), preferred_element_type=f32)


def column(row):
    return jnp.transpose(jnp.broadcast_to(row, (128, 128)))


def grid_kernel(patch_ref, far_any, near_any, taps_ref, tile_ref, right_ref, lower_ref, corner_ref,
                total, got, stage, beyond, sorted_rows, sorted_keys, taps, load_sem, stage_sem):
    loads = []
    for slot, source in enumerate((far_any, near_any)):
        load = pltpu.make_async_copy(source, got.at[pl.ds(slot * BLOCKS, BLOCKS)], load_sem.at[slot])
        load.start()
        loads.append(load)

    lane = lax.broadcasted_iota(i32, (1, 128), 1)
    keys = [(patch_ref[c:c + 1, :] * SLOTS + (lane + 128 * c)).astype(f32) for c in range(4)]
    key_columns = [column(key) for key in keys]
    ranks = []
    for key in keys:
        below = [jnp.where(other < key, 1.0, 0.0) for other in key_columns]
        ranks.append(jnp.sum(below[0] + below[1] + below[2] + below[3], axis=0, keepdims=True))
    rank_columns = [column(rank) for rank in ranks]
    for c in range(4):
        place = (lane + 128 * c).astype(f32)
        here = [jnp.where(rank_columns[d] == place, key_columns[d], 0.0) for d in range(4)]
        chosen = jnp.sum(here[0] + here[1] + here[2] + here[3], axis=0, keepdims=True)
        sorted_rows[c:c + 1, :] = chosen.astype(i32)
    load = pltpu.make_async_copy(sorted_rows, sorted_keys, load_sem.at[2])
    load.start()
    loads.append(load)

    def clear(k, carry):
        total[pl.ds(k * 4, 4)] = jnp.zeros((4, ROWS, 128), f32)
        return carry

    lax.fori_loop(0, (PATCHES + SIDE) // 4, clear, 0)

    taps[...] = jnp.zeros_like(taps)
    taps[:, 0:OVER] = taps_ref[...]
    wide = lax.broadcasted_iota(i32, (8, 128), 1)
    spread = jnp.take_along_axis(taps[...], wide // KW, axis=1)
    own = lax.broadcasted_iota(i32, (8, 128), 0) == wide % KW
    table = jnp.broadcast_to(jnp.sum(jnp.where(own, spread, 0.0), axis=0, keepdims=True), (8, 128))

    for load in loads:
        load.wait()

    row8 = lax.broadcasted_iota(i32, (8, 128), 0)
    zero = jnp.zeros((16, 128), bf16)

    def steps(cell):
        step = (cell + 7 - row8) >> 3
        return jnp.concatenate([step, step - 1], 0).astype(jnp.int16)

    def one(key):
        block = key % SLOTS
        real = got[block, 0]
        imag = got[block, 1]
        code = jnp.broadcast_to(got[block, 2], (8, 128)).astype(i32)
        cell_u = code >> 14
        cell_v = (code >> 8) & (SUB - 1)
        ku = jnp.take_along_axis(table, ((code >> 1) & 0x78) + ((row8 - cell_u) & 7), axis=1)
        kv = jnp.take_along_axis(table, ((code << 3) & 0x78) + ((row8 - cell_v) & 7), axis=1)
        step_u, step_v = steps(cell_u), steps(cell_v)
        masks_u = [step_u == jnp.int16(2 * t) for t in range(5)]
        masks_v = [step_v == jnp.int16(2 * t) for t in range(5)]

        def rows_u(first, second):
            return jnp.concatenate(
                [jnp.where(mask, value, zero) for value in (first, second) for mask in masks_u], 0)

        def rows_v(value):
            return jnp.concatenate([jnp.where(mask, value, zero) for mask in masks_v], 0)

        v_high, v_rest = halves(kv)
        r_high, r_rest = halves(ku * real)
        i_high, i_rest = halves(ku * imag)
        v_high, v_rest = rows_v(v_high), rows_v(v_rest)
        u_high, u_rest = rows_u(r_high, i_high), rows_u(r_rest, i_rest)
        out = contract(jnp.concatenate([u_high, u_rest, u_high], 1),
                       jnp.concatenate([v_high, v_high, v_rest], 1))
        patch = key // SLOTS + SIDE
        total[patch, 0:EXT, 0:80] = total[patch, 0:EXT, 0:80] + out[0:EXT]
        total[patch, EXT:ROWS, 0:80] = total[patch, EXT:ROWS, 0:80] + out[80:80 + EXT]

    lane = lax.broadcasted_iota(i32, (8, 128), 1)

    def joined(load, put):
        before = jnp.zeros((8, 128), f32)
        for pair in range(SIDE // 2):
            moved = pltpu.roll(load(2 * pair + 1), SUB, 1)
            put(pair, load(2 * pair) + jnp.where(lane >= SUB, moved, before))
            before = moved
        return jnp.where(lane < KW, before, 0.0)

    def stripe(patch_row):
        for part in range(2):
            for step in range(SUB // 8):
                start = part * EXT + step * 8

                def load(column):
                    value = total[(patch_row + 1) * SIDE + column, start:start + 8, :]
                    if step == 0:
                        last = part * EXT + SUB
                        value = value + total[patch_row * SIDE + column, last:last + 8, :]
                    return value

                def put(pair, value):
                    place = pl.multiple_of(patch_row * SUB + step * 8, 8)
                    stage[part, pl.ds(place, 8), pair * 128:pair * 128 + 128] = value

                past = joined(load, put)
                beyond[patch_row, part, step * 8:step * 8 + 8, :] = past

    def each(patch_row, carry):
        stripe(patch_row)
        for part in range(2):
            for chunk in range(CHUNKS):
                rows = pl.ds(patch_row * SUB + chunk * (SUB // CHUNKS), SUB // CHUNKS)
                pltpu.make_async_copy(stage.at[part, rows], tile_ref.at[part, rows], stage_sem).start()
        return carry

    def key_at(position):
        return sorted_keys[position // 128, position % 128]

    def several(k, done):
        for q in range(UNROLL):
            one(key_at(k * UNROLL + q))
        following = key_at(jnp.minimum((k + 1) * UNROLL, SLOTS - 1)) // (SLOTS * SIDE)
        ready = jnp.where(k == SLOTS // UNROLL - 1, SIDE, following)
        lax.fori_loop(done, ready, each, 0)
        return ready

    lax.fori_loop(0, SLOTS // UNROLL, several, 0)

    for part in range(2):
        last = part * EXT + SUB

        def load(column):
            return total[SIDE * SIDE + column, last:last + 8, :]

        def put(pair, value):
            lower_ref[part, :, pair * 128:pair * 128 + 128] = value

        corner_ref[part] = joined(load, put)
    for part in range(2):
        for step in range(SUB // 8):
            rows = slice(step * 8, step * 8 + 8)
            packed = beyond[0, part, rows, :]
            for patch_row in range(1, SIDE):
                packed = packed + pltpu.roll(beyond[patch_row, part, rows, :], patch_row * KW, 1)
            right_ref[part, rows, :] = packed
    pltpu.make_async_copy(stage, tile_ref, stage_sem).wait()


def make_tile(patches, far, near, taps):
    vmem, hbm = pl.BlockSpec(memory_space=pltpu.VMEM), pl.BlockSpec(memory_space=pl.ANY)
    return pl.pallas_call(
        grid_kernel,
        out_shape=(
            jax.ShapeDtypeStruct((2, TILE, TILE), f32), jax.ShapeDtypeStruct((2, SUB, 128), f32),
            jax.ShapeDtypeStruct((2, KW, TILE), f32), jax.ShapeDtypeStruct((2, KW, 128), f32)),
        in_specs=[vmem, hbm, hbm, vmem],
        out_specs=(hbm, vmem, vmem, vmem),
        scratch_shapes=[
            pltpu.VMEM((PATCHES + SIDE, ROWS, 128), f32),
            pltpu.VMEM((SLOTS, 3, 1, 128), f32),
            pltpu.VMEM((2, TILE, TILE), f32),
            pltpu.VMEM((SIDE, 2, SUB, 128), f32),
            pltpu.VMEM((4, 128), i32), pltpu.SMEM((4, 128), i32), pltpu.VMEM((KW, 128), f32),
            pltpu.SemaphoreType.DMA((3,)), pltpu.SemaphoreType.DMA,
        ],
        compiler_params=pltpu.CompilerParams(vmem_limit_bytes=60 << 20),
    )(patches, far, near, taps)


def margins_kernel(right_ref, lower_ref, corner_ref, left_in, upper_in, corner_in, out_sem, in_sem):
    tile, y = lax.axis_index("tile"), lax.axis_index("wp")
    tiles = ZS * XS * CORES
    barrier = pltpu.get_barrier_semaphore()
    steps = (1, TCOLS, TCOLS + 1)
    for step in steps:
        for to in ((tile + step) % tiles, (tile + tiles - step) % tiles):
            pl.semaphore_signal(barrier, inc=1, device_id=(to, y), device_id_type=MESH)
    pl.semaphore_wait(barrier, 2 * len(steps))
    copies = []
    for index, (source, target) in enumerate(
            ((right_ref, left_in), (lower_ref, upper_in), (corner_ref, corner_in))):
        copy = pltpu.make_async_remote_copy(
            src_ref=source, dst_ref=target, send_sem=out_sem.at[index], recv_sem=in_sem.at[index],
            device_id=((tile + steps[index]) % tiles, y), device_id_type=MESH)
        copy.start()
        copies.append(copy)
    for copy in copies:
        copy.wait()


def margins(right, lower, corner):
    hbm = pl.BlockSpec(memory_space=pl.ANY)
    return pl.pallas_call(
        margins_kernel,
        out_shape=tuple(jax.ShapeDtypeStruct(a.shape, a.dtype) for a in (right, lower, corner)),
        in_specs=[hbm] * 3,
        out_specs=(hbm,) * 3,
        scratch_shapes=[pltpu.SemaphoreType.DMA((3,)), pltpu.SemaphoreType.DMA((3,))],
        compiler_params=pltpu.CompilerParams(collective_id=1, has_side_effects=True, vmem_limit_bytes=60 << 20),
    )(right, lower, corner)


def finish_kernel(tile_in, left_any, upper_any, corner_any, tile_ref,
                  side, top, left_in, upper_in, corner_in, sems):
    del tile_in
    tile = lax.axis_index("tile")
    has_left = jnp.where(tile % TCOLS > 0, 1.0, 0.0).astype(f32)
    has_upper = jnp.where(tile // TCOLS > 0, 1.0, 0.0).astype(f32)
    sides = tile_ref.at[:, :, pl.ds(0, 128)]
    tops = tile_ref.at[:, pl.ds(0, KW), pl.ds(128, TILE - 128)]
    read_side = pltpu.make_async_copy(sides, side, sems.at[0])
    read_top = pltpu.make_async_copy(tops, top, sems.at[1])
    read_side.start()
    read_top.start()
    loads = []
    for index, (source, target) in enumerate(
            ((upper_any, upper_in), (left_any, left_in), (corner_any, corner_in))):
        load = pltpu.make_async_copy(source, target, sems.at[2 + index])
        load.start()
        loads.append(load)
    lane = lax.broadcasted_iota(i32, (SUB, 128), 1)
    read_top.wait()
    loads[0].wait()
    top[...] = top[...] + upper_in[:, :, 128:] * has_upper
    write_top = pltpu.make_async_copy(top, tops, sems.at[1])
    write_top.start()
    read_side.wait()
    loads[1].wait()
    loads[2].wait()
    for part in range(2):
        packed = left_in[part] * has_left
        for patch_row in range(SIDE):
            rows = slice(patch_row * SUB, patch_row * SUB + SUB)
            moved = packed if patch_row == 0 else pltpu.roll(packed, 128 - KW * patch_row, 1)
            side[part, rows, :] = side[part, rows, :] + jnp.where(lane < KW, moved, 0.0)
        side[part, 0:KW, :] = (side[part, 0:KW, :] + upper_in[part, :, 0:128] * has_upper
                               + corner_in[part] * (has_left * has_upper))
    write_side = pltpu.make_async_copy(side, sides, sems.at[0])
    write_side.start()
    write_top.wait()
    write_side.wait()


def finish(tile, left, upper, corner):
    hbm = pl.BlockSpec(memory_space=pl.ANY)
    return pl.pallas_call(
        finish_kernel,
        out_shape=jax.ShapeDtypeStruct(tile.shape, tile.dtype),
        in_specs=[hbm] * 4,
        out_specs=hbm,
        scratch_shapes=[
            pltpu.VMEM((2, TILE, 128), f32), pltpu.VMEM((2, KW, TILE - 128), f32),
            pltpu.VMEM(left.shape, f32), pltpu.VMEM(upper.shape, f32), pltpu.VMEM(corner.shape, f32),
            pltpu.SemaphoreType.DMA((5,))],
        input_output_aliases={0: 0},
        compiler_params=pltpu.CompilerParams(vmem_limit_bytes=60 << 20),
    )(tile, left, upper, corner)


def shards(visibilities, vis_weight, cell_index, tap_offsets, routes, patch_index, kernel):
    far, near, patches = exchange(
        patch_index, routes.reshape(1, BLOCKS), visibilities, vis_weight, cell_index, tap_offsets)
    tile, right, lower, corner = make_tile(
        patches, far.reshape(BLOCKS, 3, 1, 128), near.reshape(BLOCKS, 3, 1, 128), kernel.T)
    tile = finish(tile, *margins(right, lower, corner))
    return tile.reshape(1, 1, 2, TILE, TILE)


def solution(mesh):
    in_specs = (
        P(("tile", "wp"), None, None),
        P(("tile", "wp"), None),
        P(("tile", "wp"), None),
        P(("tile", "wp"), None),
        P(("tile", "wp"), None),
        P(("tile", "wp")),
        P(),
    )
    out_specs = P("wp", "tile", None, None, None)
    return jax.shard_map(shards, mesh=mesh, in_specs=in_specs, out_specs=out_specs, check_vma=False)
```
